32 devices in a mesh: freq: 4 (over y, x), shot: 8 (over z, core).
Axes of the slice: x: 2, y: 2, z: 4, core: 2. Of those that a mesh axis runs over, the one named last changes fastest.
Arguments:
- up_traces: bfloat16 [512, 128, 1024], P(('freq', 'shot')), may hold values from -6 to 6
- down_traces: bfloat16 [512, 128, 1024], P(('freq', 'shot')), may hold values from -6 to 6
Outputs:
- reflectivity: float32 [4, 1024, 2, 1024], P('freq', 'shot')
The draws below stay inside these ranges and needn't reach their ends.
All inputs are finite; a program needn't handle non-finite values.
Results may differ from the reference program's by a relative error of at most 0.0054.
Values may be sent and summed in bfloat16 or wider, within the bound.
No kernel may reach another device: no remote copies, remote signals or barrier semaphores. Data moves between devices by JAX's collectives and lax.ppermute only.
A program may use at most 128 MiB of HBM per device.

```python
import math
import jax
import jax.numpy as jnp
from jax import lax

R = 1024
NT = 128
ITERS = 2
SHOTS = 512
FIRST_BIN = 8
N_FREQ = 4


def raised(result, own_key, source, target, parts, factor):
    owner, partner = [(jnp.arange(result.shape[dim]) // (result.shape[dim] // parts)).reshape([-1 if axis == dim else 1 for axis in range(result.ndim)]) for dim in (source, target)]
    chosen = jax.random.permutation(own_key, parts)[partner]
    strong = (owner == chosen) | (owner == (partner + parts // 2) % parts)
    return jnp.where(strong, factor * result, result)


def block_levels(rng, dims, pieces, smallest, high):
    loudness = 1.0
    for position, blocks in pieces:
        heights = jax.random.uniform(jax.random.fold_in(jax.random.fold_in(rng, 6), position), (blocks,), jnp.float32, smallest / len(pieces), high / len(pieces))
        loudness = loudness * jnp.repeat(jnp.exp(heights), dims[position] // blocks).reshape((-1,) + (1,) * (len(dims) - 1 - position))
    return loudness


def normal_values(key, shape, deviation, bound, cuts=(), held_as=jnp.bfloat16):
    values = deviation * jax.random.normal(key, shape, jnp.float32)
    if cuts:
        values = values * block_levels(key, shape, cuts, -0.22, 0.18)
    return jnp.clip(values, -bound, bound).astype(held_as)


def gaussian_with(stream_key, shape, scale, most, shards, heavy, kind=jnp.bfloat16):
    array = scale * jax.random.normal(stream_key, shape, jnp.float32)
    if shards:
        array = array * block_levels(stream_key, shape, shards, -0.22, 0.18)
    return jnp.clip(raised(array, jax.random.fold_in(stream_key, 3), *heavy), -most, most).astype(kind)


def setup_inputs(seed: int = 0) -> dict:
    key_of = jax.random.split(jax.random.key(seed), 3)
    return {
        "up_traces": normal_values(key_of[0], (SHOTS, NT, R), 1.0, 6.0, ((0, 32),)),
        "down_traces": gaussian_with(key_of[1], (SHOTS, NT, R), 1.0, 6.0, ((0, 32),), (0, 2, 32, 2.75)),
    }


def make_table(samples, nfreq, first):
    times = jnp.arange(samples, dtype=jnp.int32)
    bins = first + jnp.arange(nfreq, dtype=jnp.int32)
    phase = (times[:, None] * bins[None, :]) % samples
    angle = 2.0 * math.pi * phase.astype(jnp.float32) / samples
    return jnp.stack([jnp.cos(angle), -jnp.sin(angle)], -1).astype(jnp.bfloat16)


def spectra(traces, table):
    return jnp.einsum("str,tfc->sfcr", traces.astype(jnp.float32), table.astype(jnp.float32)).astype(jnp.bfloat16)


def hidot(left, right):
    return jnp.dot(left, right, precision=lax.Precision.HIGHEST, preferred_element_type=jnp.float32)


def solve_one(down_one, up_one):
    down_re, down_im = down_one[:, 0, :], down_one[:, 1, :]
    up_re, up_im = up_one[:, 0, :], up_one[:, 1, :]
    gram_re = jnp.dot(down_re.T, down_re, preferred_element_type=jnp.float32) + jnp.dot(down_im.T, down_im, preferred_element_type=jnp.float32)
    gram_im = jnp.dot(down_im.T, down_re, preferred_element_type=jnp.float32) - jnp.dot(down_re.T, down_im, preferred_element_type=jnp.float32)
    rhs_re = jnp.dot(down_re.T, up_re, preferred_element_type=jnp.float32) + jnp.dot(down_im.T, up_im, preferred_element_type=jnp.float32)
    rhs_im = jnp.dot(down_im.T, up_re, preferred_element_type=jnp.float32) - jnp.dot(down_re.T, up_im, preferred_element_type=jnp.float32)
    damping = 0.1 * jnp.trace(gram_re) / R

    def apply(dir_re, dir_im):
        img_re = hidot(gram_re, dir_re) - hidot(gram_im, dir_im) + damping * dir_re
        img_im = hidot(gram_re, dir_im) + hidot(gram_im, dir_re) + damping * dir_im
        return img_re, img_im

    sol_re = jnp.zeros_like(rhs_re)
    sol_im = jnp.zeros_like(rhs_im)
    res_re, res_im = rhs_re, rhs_im
    dir_re, dir_im = rhs_re, rhs_im
    norm_now = jnp.sum(res_re * res_re + res_im * res_im, axis=0)
    for step in range(ITERS):
        img_re, img_im = apply(dir_re, dir_im)
        curv = jnp.sum(dir_re * img_re + dir_im * img_im, axis=0)
        alpha = norm_now / curv
        sol_re = sol_re + alpha * dir_re
        sol_im = sol_im + alpha * dir_im
        res_re = res_re - alpha * img_re
        res_im = res_im - alpha * img_im
        if step + 1 < ITERS:
            norm_next = jnp.sum(res_re * res_re + res_im * res_im, axis=0)
            ratio = norm_next / norm_now
            dir_re = res_re + ratio * dir_re
            dir_im = res_im + ratio * dir_im
            norm_now = norm_next
    return jnp.stack([sol_re, sol_im], 1)


def reference(up_traces, down_traces):
    table = make_table(NT, N_FREQ, FIRST_BIN)
    up_spec = spectra(up_traces, table)
    down_spec = spectra(down_traces, table)
    outputs = [solve_one(down_spec[:, f], up_spec[:, f]) for f in range(N_FREQ)]
    return jnp.stack(outputs, 0)
```

```python
import math

import jax
import jax.numpy as jnp
from jax import lax
from jax.sharding import Mesh, PartitionSpec as P


def make_table(samples, nfreq, first):
    times = jnp.arange(samples, dtype=jnp.int32)
    bins = first + jnp.arange(nfreq, dtype=jnp.int32)
    phase = times[:, None] * bins[None, :] % samples
    angle = 2.0 * math.pi * phase.astype(jnp.float32) / samples
    return jnp.stack([jnp.cos(angle), -jnp.sin(angle)], -1).astype(jnp.bfloat16)


def ring_order(chips):
    return [0, 1, 3, 2] if chips == 4 else list(range(chips))


def ring_gather(piece, chips):
    order = ring_order(chips)
    pairs = [(order[i], order[(i + 1) % chips]) for i in range(chips)]
    pieces = [piece]
    for _ in range(chips - 1):
        pieces.append(lax.ppermute(pieces[-1], "chip", pairs))
    return pieces


def swap_core(array):
    return lax.ppermute(array, "core", [(0, 1), (1, 0)])


def split(array):
    high = lax.reduce_precision(array, 8, 7)
    return high.astype(jnp.bfloat16), (array - high).astype(jnp.bfloat16)


def dot(left, right):
    return jnp.dot(left, right, preferred_element_type=jnp.float32)


def dot_t(left, right):
    return lax.dot_general(left, right, (((0,), (0,)), ((), ())), preferred_element_type=jnp.float32)


def spectra(traces, table):
    return jnp.einsum("str,tfc->fcsr", traces, table, preferred_element_type=jnp.float32).astype(jnp.bfloat16)


def to_freq(spec):
    return lax.all_to_all(spec, "freq", split_axis=0, concat_axis=0, tiled=True)


def shards(up_traces, down_traces):
    local_shots, samples, width = up_traces.shape
    nfreq, chips = lax.axis_size("freq"), lax.axis_size("chip")
    core = lax.axis_index("core")
    half = width // 2
    rows = width // (2 * chips)
    table = make_table(samples, nfreq, samples // 16)

    down = to_freq(spectra(down_traces, table))
    own = ring_gather(down, chips)
    down_all = jnp.stack([jnp.stack([piece, swap_core(piece)]) for piece in own])

    up = to_freq(spectra(up_traces, table))
    mine = lax.dynamic_slice_in_dim(up, core * half, half, 3)
    theirs = swap_core(lax.dynamic_slice_in_dim(up, (1 - core) * half, half, 3))
    up_all = jnp.stack(ring_gather(jnp.stack([mine, theirs]), chips))

    even = down_all.reshape(-1, width)
    odd = jnp.stack([-down_all[:, :, :, 1], down_all[:, :, :, 0]], 3).reshape(-1, width)
    start = up_all.reshape(-1, half)

    gram = lax.dot_general(even, even, (((1,), (1,)), ((), ())), preferred_element_type=jnp.float32) + lax.dot_general(
        odd, odd, (((1,), (1,)), ((), ())), preferred_element_type=jnp.float32
    )
    damping = 0.05 * jnp.trace(gram) / width
    gram_high, gram_low = split(gram)

    start_wide = start.astype(jnp.float32)
    image = dot(gram_high, start) + dot(gram_low, start)
    norm_now = jnp.sum(start_wide * image, axis=0)
    alpha = norm_now / (jnp.sum(image * image, axis=0) + damping * norm_now)
    resid = (1.0 - alpha * damping) * start_wide - alpha * image
    resid_image = dot(gram_high, resid.astype(jnp.bfloat16))
    norm_next = jnp.sum(resid * resid_image, axis=0)
    ratio = norm_next / norm_now
    direc = resid + ratio * start_wide
    direc_image = resid_image + ratio * image
    curv = jnp.sum(direc_image * direc_image, axis=0) + damping * jnp.sum(direc * direc_image, axis=0)
    weights = alpha * start_wide + norm_next / curv * direc
    weights_high, weights_low = split(weights)

    chip = lax.axis_index("chip")
    even_rows = lax.dynamic_slice_in_dim(even, chip * 2 * rows, 2 * rows, 1)
    odd_rows = lax.dynamic_slice_in_dim(odd, chip * 2 * rows, 2 * rows, 1)
    real = dot_t(even_rows, weights_high) + dot_t(even_rows, weights_low)
    imag = -(dot_t(odd_rows, weights_high) + dot_t(odd_rows, weights_low))
    block = jnp.stack([real, imag], 1)
    kept = lax.dynamic_slice_in_dim(block, core * rows, rows, 0)
    got = swap_core(lax.dynamic_slice_in_dim(block, (1 - core) * rows, rows, 0))
    first = core == 0
    return jnp.concatenate([jnp.where(first, kept, got), jnp.where(first, got, kept)], 2)[None]


def solution(mesh):
    nfreq, nshot = mesh.devices.shape
    fine = Mesh(mesh.devices.reshape(nfreq, nshot // 2, 2), ("freq", "chip", "core"))
    spec = P(("freq", "chip", "core"), None, None)
    out_specs = P("freq", ("chip", "core"), None, None)
    return jax.shard_map(shards, mesh=fine, in_specs=(spec, spec), out_specs=out_specs, check_vma=False)
```

```python
import functools
import math

import jax
import jax.numpy as jnp
import numpy as np
from jax import lax
from jax.experimental import pallas as pl
from jax.experimental.pallas import tpu as pltpu
from jax.sharding import Mesh, PartitionSpec as P

CHUNK = 256
LIMIT = 48 * 1024 * 1024


def make_table(samples, nfreq, first):
    times = np.arange(samples)
    phase = times[:, None] * (first + np.arange(nfreq))[None, :] % samples
    angle = np.float32(2.0 * math.pi) * phase.astype(np.float32) / np.float32(samples)
    return np.stack([np.cos(angle), -np.sin(angle)], -1).astype(jnp.bfloat16)


def spread_table(samples, nfreq, shots):
    table = make_table(samples, nfreq, samples // 16).astype(np.float32)
    whole = np.einsum("tfc,sz->fcszt", table, np.eye(shots, dtype=np.float32))
    return whole.reshape(nfreq * 2 * shots, shots * samples).astype(jnp.bfloat16)


def ring_order(chips):
    return [0, 1, 3, 2] if chips == 4 else list(range(chips))


def ring_gather(piece, chips):
    order = ring_order(chips)
    pairs = [(order[i], order[(i + 1) % chips]) for i in range(chips)]
    pieces = [piece]
    for _ in range(chips - 1):
        pieces.append(lax.ppermute(pieces[-1], "chip", pairs))
    return pieces


def swap_core(array):
    return lax.ppermute(array, "core", [(0, 1), (1, 0)])


def split(array):
    high = lax.reduce_precision(array, 8, 7)
    return high.astype(jnp.bfloat16), (array - high).astype(jnp.bfloat16)


def dot(left, right):
    return jnp.dot(left, right, preferred_element_type=jnp.float32)


def dot_nt(left, right):
    return lax.dot_general(left, right, (((1,), (1,)), ((), ())), preferred_element_type=jnp.float32)


def spectra(traces, matrix):
    return dot(matrix, traces.reshape(-1, traces.shape[2])).astype(jnp.bfloat16)


def to_freq(spec, nfreq):
    parts = spec.reshape(nfreq, -1, spec.shape[1])
    me = lax.axis_index("freq")
    out = []
    for step in range(nfreq):
        there = me ^ step
        part = lax.dynamic_index_in_dim(parts, there, 0, keepdims=False)
        out.append(part if step == 0 else lax.ppermute(part, "freq", [(f, f ^ step) for f in range(nfreq)]))
    return jnp.concatenate(out, 0)


def gram_kernel(shots, place, *refs):
    pieces, (high, low, damping, rows_t), (both,) = refs[:-5], refs[-5:-1], refs[-1:]
    width = pieces[0].shape[1]
    count = pieces[0].shape[0]
    total = jnp.zeros((1, width), jnp.float32)
    for number, piece in enumerate(pieces):
        block = piece[...]
        wide = block.astype(jnp.float32)
        total = total + jnp.sum(wide * wide, axis=0, keepdims=True)
        at = number * count
        both[pl.ds(at, count), pl.ds(0, width)] = block
        for part in range(0, count, 2 * shots):
            both[pl.ds(at + part, shots), pl.ds(width, width)] = -block[part + shots : part + 2 * shots]
            both[pl.ds(at + part + shots, shots), pl.ds(width, width)] = block[part : part + shots]
    damping[...] = 0.1 * jnp.sum(total, axis=1, keepdims=True) / width
    size = both.shape[0]
    for at in range(0, size, 256):
        gram = dot_nt(both[pl.ds(at, 256), :], both[...])
        rounded = gram.astype(jnp.bfloat16)
        high[pl.ds(at, 256), :] = rounded
        low[pl.ds(at, 256), :] = (gram - rounded.astype(jnp.float32)).astype(jnp.bfloat16)
    wide = rows_t.shape[0] // 4
    for number in range(2):
        start = pl.multiple_of(place[number] * wide, wide)
        rows_t[pl.ds(2 * number * wide, wide), :] = both[:, pl.ds(start, wide)].T
        rows_t[pl.ds((2 * number + 1) * wide, wide), :] = -both[:, pl.ds(width + start, wide)].T


def gram_call(place, pieces, shots, rows):
    count, width = pieces[0].shape
    size = count * len(pieces)
    square = jax.ShapeDtypeStruct((size, size), jnp.bfloat16)
    return pl.pallas_call(
        functools.partial(gram_kernel, shots),
        out_shape=(
            square,
            square,
            jax.ShapeDtypeStruct((1, 1), jnp.float32),
            jax.ShapeDtypeStruct((4 * rows, size), jnp.bfloat16),
        ),
        in_specs=[pl.BlockSpec(memory_space=pltpu.SMEM)] + [pl.BlockSpec(memory_space=pltpu.VMEM)] * len(pieces),
        out_specs=(pl.BlockSpec(memory_space=pltpu.VMEM),) * 4,
        scratch_shapes=[pltpu.VMEM((size, 2 * width), jnp.bfloat16)],
        compiler_params=pltpu.CompilerParams(vmem_limit_bytes=LIMIT),
        cost_estimate=pl.CostEstimate(flops=4 * size * size * width, bytes_accessed=4 * size * size, transcendentals=0),
        name="gram",
    )(place, *pieces)


def solve_kernel(high, low, damping, rows_t, *refs):
    pieces, (kept, sent), (start, image, step_high, step_low, step_image) = refs[:-7], refs[-7:-5], refs[-5:]
    size, columns = start.shape
    tiles = [pl.ds(at, 256) for at in range(0, size, 256)]
    count = pieces[0].shape[0]
    for number, piece in enumerate(pieces):
        start[pl.ds(number * count, count), :] = piece[...]
    damp = damping[...]
    norm_now = jnp.zeros((1, columns), jnp.float32)
    image_norm = jnp.zeros((1, columns), jnp.float32)
    for tile in tiles:
        value = dot(high[tile, :], start[...]) + dot(low[tile, :], start[...])
        image[tile, :] = value
        norm_now += jnp.sum(start[tile, :].astype(jnp.float32) * value, axis=0, keepdims=True)
        image_norm += jnp.sum(value * value, axis=0, keepdims=True)
    alpha = norm_now / (image_norm + damp * norm_now)
    keep = 1.0 - alpha * damp
    for tile in tiles:
        resid = keep * start[tile, :].astype(jnp.float32) - alpha * image[tile, :]
        rounded = resid.astype(jnp.bfloat16)
        step_high[tile, :] = rounded
        step_low[tile, :] = (resid - rounded.astype(jnp.float32)).astype(jnp.bfloat16)
    norm_next = jnp.zeros((1, columns), jnp.float32)
    for tile in tiles:
        value = dot(high[tile, :], step_high[...]) + (
            dot(low[tile, :], step_high[...]) + dot(high[tile, :], step_low[...])
        )
        step_image[tile, :] = value
        resid = keep * start[tile, :].astype(jnp.float32) - alpha * image[tile, :]
        norm_next += jnp.sum(resid * value, axis=0, keepdims=True)
    ratio = norm_next / norm_now
    curv = jnp.zeros((1, columns), jnp.float32)
    for tile in tiles:
        direc = (keep + ratio) * start[tile, :].astype(jnp.float32) - alpha * image[tile, :]
        value = step_image[tile, :] + ratio * image[tile, :]
        curv += jnp.sum(value * (value + damp * direc), axis=0, keepdims=True)
    beta = norm_next / curv
    from_start = alpha + beta * (keep + ratio)
    from_image = alpha * beta
    for tile in tiles:
        weight = from_start * start[tile, :].astype(jnp.float32) - from_image * image[tile, :]
        rounded = weight.astype(jnp.bfloat16)
        step_high[tile, :] = rounded
        step_low[tile, :] = (weight - rounded.astype(jnp.float32)).astype(jnp.bfloat16)
    rows = rows_t.shape[0] // 4
    for number, out in enumerate((kept, sent)):
        for part in range(2):
            left = rows_t[pl.ds((2 * number + part) * rows, rows), :]
            out[part] = dot(left, step_high[...]) + dot(left, step_low[...])


def solve_call(high, low, damping, rows_t, pieces):
    size = high.shape[0]
    columns = pieces[0].shape[1]
    rows = rows_t.shape[0] // 4
    block = jax.ShapeDtypeStruct((2, rows, columns), jnp.float32)
    return pl.pallas_call(
        solve_kernel,
        out_shape=(block, block),
        in_specs=[pl.BlockSpec(memory_space=pltpu.VMEM)] * (4 + len(pieces)),
        out_specs=(pl.BlockSpec(memory_space=pltpu.VMEM),) * 2,
        scratch_shapes=[
            pltpu.VMEM((size, columns), jnp.bfloat16),
            pltpu.VMEM((size, columns), jnp.float32),
            pltpu.VMEM((size, columns), jnp.bfloat16),
            pltpu.VMEM((size, columns), jnp.bfloat16),
            pltpu.VMEM((size, columns), jnp.float32),
        ],
        compiler_params=pltpu.CompilerParams(vmem_limit_bytes=LIMIT),
        cost_estimate=pl.CostEstimate(flops=12 * size * size * columns, bytes_accessed=4 * size * size, transcendentals=0),
        name="solve",
    )(high, low, damping, rows_t, *pieces)


def plain_gram(place, pieces, shots, rows):
    width = pieces[0].shape[1]
    even = jnp.concatenate(pieces, 0)
    turned = even.reshape(-1, 2, shots, width)
    odd = jnp.stack([-turned[:, 1], turned[:, 0]], 1).reshape(even.shape)
    blocks = []
    for number in range(2):
        blocks.append(lax.dynamic_slice_in_dim(even, place[number] * rows, rows, 1).T)
        blocks.append(-lax.dynamic_slice_in_dim(odd, place[number] * rows, rows, 1).T)
    return even, odd, 0.1 * jnp.sum(jnp.square(even.astype(jnp.float32))) / width, jnp.concatenate(blocks, 0)


def dot_tn(left, right):
    return lax.dot_general(left, right, (((0,), (0,)), ((), ())), preferred_element_type=jnp.float32)


def plain_apply(even, odd, parts):
    out = []
    for side in (even, odd):
        high, low = split(sum(dot_tn(side, part) for part in parts))
        out.append(dot(side, high) + dot(side, low))
    return out[0] + out[1]


def plain_solve(even, odd, damping, rows_t, pieces):
    start = jnp.concatenate(pieces, 0)
    wide = start.astype(jnp.float32)
    image = plain_apply(even, odd, (start,))
    norm_now = jnp.sum(wide * image, axis=0)
    alpha = norm_now / (jnp.sum(image * image, axis=0) + damping * norm_now)
    resid = (1.0 - alpha * damping) * wide - alpha * image
    resid_image = plain_apply(even, odd, split(resid))
    norm_next = jnp.sum(resid * resid_image, axis=0)
    ratio = norm_next / norm_now
    direc = resid + ratio * wide
    direc_image = resid_image + ratio * image
    curv = jnp.sum(direc_image * (direc_image + damping * direc), axis=0)
    weights_high, weights_low = split(alpha * wide + norm_next / curv * direc)
    block = (dot(rows_t, weights_high) + dot(rows_t, weights_low)).reshape(2, 2, -1, start.shape[1])
    return block[0], block[1]


def shards(up_traces, down_traces):
    local_shots, samples, width = up_traces.shape
    nfreq, chips = lax.axis_size("freq"), lax.axis_size("chip")
    core = lax.axis_index("core")
    half = width // 2
    rows = width // (2 * chips)
    size = 2 * local_shots * nfreq * 2 * chips
    matrix = jnp.asarray(spread_table(samples, nfreq, local_shots))

    down = to_freq(spectra(down_traces, matrix), nfreq)
    own = ring_gather(down, chips)
    pieces = []
    for piece in own:
        pieces += [piece, swap_core(piece)]

    up = to_freq(spectra(up_traces, matrix), nfreq)
    mine = lax.dynamic_slice_in_dim(up, core * half, half, 1)
    theirs = swap_core(lax.dynamic_slice_in_dim(up, (1 - core) * half, half, 1))
    up = jnp.concatenate([mine, theirs], 0)

    place = 2 * lax.axis_index("chip") + jnp.stack([core, 1 - core]).astype(jnp.int32)
    small = size <= 1024 and rows % 128 == 0 and half % CHUNK == 0 and local_shots % 16 == 0
    gram, solve = (gram_call, solve_call) if small else (plain_gram, plain_solve)
    operator = gram(place, pieces, local_shots, rows)
    chunk = CHUNK if half % CHUNK == 0 else half
    kept, got = [], []
    for at in range(0, half, chunk):
        stay, send = solve(*operator, ring_gather(up[:, at : at + chunk], chips))
        kept.append(stay)
        got.append(swap_core(send))
    kept, got = jnp.concatenate(kept, 2), jnp.concatenate(got, 2)
    first = core == 0
    block = jnp.concatenate([jnp.where(first, kept, got), jnp.where(first, got, kept)], 2)
    return jnp.transpose(block, (1, 0, 2))[None]


def solution(mesh):
    nfreq, nshot = mesh.devices.shape
    fine = Mesh(mesh.devices.reshape(nfreq, nshot // 2, 2), ("freq", "chip", "core"))
    spec = P(("freq", "chip", "core"), None, None)
    out_specs = P("freq", ("chip", "core"), None, None)
    return jax.shard_map(shards, mesh=fine, in_specs=(spec, spec), out_specs=out_specs, check_vma=False)
```

```python
import functools
import math

import jax
import jax.numpy as jnp
import numpy as np
from jax import lax
from jax.experimental import pallas as pl
from jax.experimental.pallas import tpu as pltpu
from jax.sharding import Mesh, PartitionSpec as P

CHUNK = 256
LIMIT = 48 * 1024 * 1024


def make_table(samples, nfreq, first):
    times = np.arange(samples)
    phase = times[:, None] * (first + np.arange(nfreq))[None, :] % samples
    angle = np.float32(2.0 * math.pi) * phase.astype(np.float32) / np.float32(samples)
    return np.stack([np.cos(angle), -np.sin(angle)], -1).astype(jnp.bfloat16)


def spread_table(samples, nfreq, shots):
    table = make_table(samples, nfreq, samples // 16).astype(np.float32)
    whole = np.einsum("tfc,sz->fcszt", table, np.eye(shots, dtype=np.float32))
    return whole.reshape(nfreq * 2 * shots, shots * samples).astype(jnp.bfloat16)


def ring_order(chips):
    return [0, 1, 3, 2] if chips == 4 else list(range(chips))


def ring_gather(piece, chips):
    order = ring_order(chips)
    pairs = [(order[i], order[(i + 1) % chips]) for i in range(chips)]
    pieces = [piece]
    for _ in range(chips - 1):
        pieces.append(lax.ppermute(pieces[-1], "chip", pairs))
    return pieces


def after(array, *others):
    return lax.optimization_barrier((array, *others))[0]


def swap_core(array):
    return lax.ppermute(array, "core", [(0, 1), (1, 0)])


def split(array):
    high = lax.reduce_precision(array, 8, 7)
    return high.astype(jnp.bfloat16), (array - high).astype(jnp.bfloat16)


def dot(left, right):
    return jnp.dot(left, right, preferred_element_type=jnp.float32)


def dot_nt(left, right):
    return lax.dot_general(left, right, (((1,), (1,)), ((), ())), preferred_element_type=jnp.float32)


def spectra(traces, matrix):
    return dot(matrix, traces.reshape(-1, traces.shape[2])).astype(jnp.bfloat16)


def to_freq(spec, nfreq):
    parts = spec.reshape(nfreq, -1, spec.shape[1])
    me = lax.axis_index("freq")
    out = []
    for step in range(nfreq):
        there = me ^ step
        part = lax.dynamic_index_in_dim(parts, there, 0, keepdims=False)
        out.append(part if step == 0 else lax.ppermute(part, "freq", [(f, f ^ step) for f in range(nfreq)]))
    return jnp.concatenate(out, 0)


def gram_kernel(shots, place, *refs):
    pieces, (high, low, damping, rows_t), (both,) = refs[:-5], refs[-5:-1], refs[-1:]
    width = pieces[0].shape[1]
    count = pieces[0].shape[0]
    total = jnp.zeros((1, width), jnp.float32)
    for number, piece in enumerate(pieces):
        block = piece[...]
        wide = block.astype(jnp.float32)
        total = total + jnp.sum(wide * wide, axis=0, keepdims=True)
        at = number * count
        both[pl.ds(at, count), pl.ds(0, width)] = block
        for part in range(0, count, 2 * shots):
            both[pl.ds(at + part, shots), pl.ds(width, width)] = -block[part + shots : part + 2 * shots]
            both[pl.ds(at + part + shots, shots), pl.ds(width, width)] = block[part : part + shots]
    damping[...] = 0.1 * jnp.sum(total, axis=1, keepdims=True) / width
    size = both.shape[0]
    for at in range(0, size, 256):
        gram = dot_nt(both[pl.ds(at, 256), :], both[...])
        rounded = gram.astype(jnp.bfloat16)
        high[pl.ds(at, 256), :] = rounded
        low[pl.ds(at, 256), :] = (gram - rounded.astype(jnp.float32)).astype(jnp.bfloat16)
    wide = rows_t.shape[0] // 8
    for number in range(4):
        start = pl.multiple_of(place[number] * wide, wide)
        rows_t[pl.ds(2 * number * wide, wide), :] = both[:, pl.ds(start, wide)].T
        rows_t[pl.ds((2 * number + 1) * wide, wide), :] = -both[:, pl.ds(width + start, wide)].T


def gram_call(place, pieces, shots, rows):
    count, width = pieces[0].shape
    size = count * len(pieces)
    square = jax.ShapeDtypeStruct((size, size), jnp.bfloat16)
    return pl.pallas_call(
        functools.partial(gram_kernel, shots),
        out_shape=(
            square,
            square,
            jax.ShapeDtypeStruct((1, 1), jnp.float32),
            jax.ShapeDtypeStruct((8 * rows, size), jnp.bfloat16),
        ),
        in_specs=[pl.BlockSpec(memory_space=pltpu.SMEM)] + [pl.BlockSpec(memory_space=pltpu.VMEM)] * len(pieces),
        out_specs=(pl.BlockSpec(memory_space=pltpu.VMEM),) * 4,
        scratch_shapes=[pltpu.VMEM((size, 2 * width), jnp.bfloat16)],
        compiler_params=pltpu.CompilerParams(vmem_limit_bytes=LIMIT),
        cost_estimate=pl.CostEstimate(flops=4 * size * size * width, bytes_accessed=4 * size * size, transcendentals=0),
        name="gram",
    )(place, *pieces)


def solve_kernel(high, low, damping, rows_t, *refs):
    pieces, outs, (start, image, step_high, step_low, step_image) = refs[:-9], refs[-9:-5], refs[-5:]
    size, columns = start.shape
    tiles = [pl.ds(at, 256) for at in range(0, size, 256)]
    count = pieces[0].shape[0]
    for number, piece in enumerate(pieces):
        start[pl.ds(number * count, count), :] = piece[...]
    damp = damping[...]
    norm_now = jnp.zeros((1, columns), jnp.float32)
    image_norm = jnp.zeros((1, columns), jnp.float32)
    for tile in tiles:
        value = dot(high[tile, :], start[...]) + dot(low[tile, :], start[...])
        image[tile, :] = value
        norm_now += jnp.sum(start[tile, :].astype(jnp.float32) * value, axis=0, keepdims=True)
        image_norm += jnp.sum(value * value, axis=0, keepdims=True)
    alpha = norm_now / (image_norm + damp * norm_now)
    keep = 1.0 - alpha * damp
    for tile in tiles:
        resid = keep * start[tile, :].astype(jnp.float32) - alpha * image[tile, :]
        rounded = resid.astype(jnp.bfloat16)
        step_high[tile, :] = rounded
        step_low[tile, :] = (resid - rounded.astype(jnp.float32)).astype(jnp.bfloat16)
    norm_next = jnp.zeros((1, columns), jnp.float32)
    for tile in tiles:
        value = dot(high[tile, :], step_high[...]) + (
            dot(low[tile, :], step_high[...]) + dot(high[tile, :], step_low[...])
        )
        step_image[tile, :] = value
        resid = keep * start[tile, :].astype(jnp.float32) - alpha * image[tile, :]
        norm_next += jnp.sum(resid * value, axis=0, keepdims=True)
    ratio = norm_next / norm_now
    curv = jnp.zeros((1, columns), jnp.float32)
    for tile in tiles:
        direc = (keep + ratio) * start[tile, :].astype(jnp.float32) - alpha * image[tile, :]
        value = step_image[tile, :] + ratio * image[tile, :]
        curv += jnp.sum(value * (value + damp * direc), axis=0, keepdims=True)
    beta = norm_next / curv
    from_start = alpha + beta * (keep + ratio)
    from_image = alpha * beta
    for tile in tiles:
        weight = from_start * start[tile, :].astype(jnp.float32) - from_image * image[tile, :]
        rounded = weight.astype(jnp.bfloat16)
        step_high[tile, :] = rounded
        step_low[tile, :] = (weight - rounded.astype(jnp.float32)).astype(jnp.bfloat16)
    rows = rows_t.shape[0] // 8
    for number, out in enumerate(outs):
        for part in range(2):
            left = rows_t[pl.ds((2 * number + part) * rows, rows), :]
            out[part] = (dot(left, step_high[...]) + dot(left, step_low[...])).astype(out.dtype)


def solve_call(high, low, damping, rows_t, pieces):
    size = high.shape[0]
    columns = pieces[0].shape[1]
    rows = rows_t.shape[0] // 8
    block = jax.ShapeDtypeStruct((2, rows, columns), jnp.float32)
    rounded = jax.ShapeDtypeStruct((2, rows, columns), jnp.bfloat16)
    return pl.pallas_call(
        solve_kernel,
        out_shape=(block, block, rounded, rounded),
        in_specs=[pl.BlockSpec(memory_space=pltpu.VMEM)] * (4 + len(pieces)),
        out_specs=(pl.BlockSpec(memory_space=pltpu.VMEM),) * 4,
        scratch_shapes=[
            pltpu.VMEM((size, columns), jnp.bfloat16),
            pltpu.VMEM((size, columns), jnp.float32),
            pltpu.VMEM((size, columns), jnp.bfloat16),
            pltpu.VMEM((size, columns), jnp.bfloat16),
            pltpu.VMEM((size, columns), jnp.float32),
        ],
        compiler_params=pltpu.CompilerParams(vmem_limit_bytes=LIMIT),
        cost_estimate=pl.CostEstimate(flops=12 * size * size * columns, bytes_accessed=4 * size * size, transcendentals=0),
        name="solve",
    )(high, low, damping, rows_t, *pieces)


def plain_gram(place, pieces, shots, rows):
    width = pieces[0].shape[1]
    even = jnp.concatenate(pieces, 0)
    turned = even.reshape(-1, 2, shots, width)
    odd = jnp.stack([-turned[:, 1], turned[:, 0]], 1).reshape(even.shape)
    blocks = []
    for number in range(2):
        blocks.append(lax.dynamic_slice_in_dim(even, place[number] * rows, rows, 1).T)
        blocks.append(-lax.dynamic_slice_in_dim(odd, place[number] * rows, rows, 1).T)
    return even, odd, 0.1 * jnp.sum(jnp.square(even.astype(jnp.float32))) / width, jnp.concatenate(blocks, 0)


def dot_tn(left, right):
    return lax.dot_general(left, right, (((0,), (0,)), ((), ())), preferred_element_type=jnp.float32)


def plain_apply(even, odd, parts):
    out = []
    for side in (even, odd):
        high, low = split(sum(dot_tn(side, part) for part in parts))
        out.append(dot(side, high) + dot(side, low))
    return out[0] + out[1]


def plain_solve(even, odd, damping, rows_t, pieces):
    start = jnp.concatenate(pieces, 0)
    wide = start.astype(jnp.float32)
    image = plain_apply(even, odd, (start,))
    norm_now = jnp.sum(wide * image, axis=0)
    alpha = norm_now / (jnp.sum(image * image, axis=0) + damping * norm_now)
    resid = (1.0 - alpha * damping) * wide - alpha * image
    resid_image = plain_apply(even, odd, split(resid))
    norm_next = jnp.sum(resid * resid_image, axis=0)
    ratio = norm_next / norm_now
    direc = resid + ratio * wide
    direc_image = resid_image + ratio * image
    curv = jnp.sum(direc_image * (direc_image + damping * direc), axis=0)
    weights_high, weights_low = split(alpha * wide + norm_next / curv * direc)
    block = (dot(rows_t, weights_high) + dot(rows_t, weights_low)).reshape(2, 2, -1, start.shape[1])
    return block[0], block[1]


def ring_shards(up_traces, down_traces):
    local_shots, samples, width = up_traces.shape
    nfreq, chips = lax.axis_size("freq"), lax.axis_size("chip")
    core = lax.axis_index("core")
    half = width // 2
    rows = width // (2 * chips)
    matrix = jnp.asarray(spread_table(samples, nfreq, local_shots))

    down = to_freq(spectra(down_traces, matrix), nfreq)
    own = ring_gather(down, chips)
    pieces = []
    for piece in own:
        pieces += [piece, swap_core(piece)]

    up = to_freq(spectra(up_traces, matrix), nfreq)
    mine = lax.dynamic_slice_in_dim(up, core * half, half, 1)
    theirs = swap_core(lax.dynamic_slice_in_dim(up, (1 - core) * half, half, 1))
    up = jnp.concatenate([mine, theirs], 0)

    place = 2 * lax.axis_index("chip") + jnp.stack([core, 1 - core]).astype(jnp.int32)
    operator = plain_gram(place, pieces, local_shots, rows)
    chunk = CHUNK if half % CHUNK == 0 else half
    kept, got = [], []
    for at in range(0, half, chunk):
        stay, send = plain_solve(*operator, ring_gather(up[:, at : at + chunk], chips))
        kept.append(stay)
        got.append(swap_core(send))
    kept, got = jnp.concatenate(kept, 2), jnp.concatenate(got, 2)
    first = core == 0
    block = jnp.concatenate([jnp.where(first, kept, got), jnp.where(first, got, kept)], 2)
    return jnp.transpose(block, (1, 0, 2))[None]


def spectra_kernel(steps, down_traces, up_traces, matrix, *refs):
    outs, (traces, turned, arrived) = refs[:steps], refs[steps:]
    me = lax.axis_index("freq")
    depth = traces.shape[2]
    copies = []
    for side, source in enumerate((down_traces, up_traces)):
        for part in range(traces.shape[1]):
            copy = pltpu.make_async_copy(
                source.at[pl.ds(part * depth, depth)], traces.at[side, part], arrived.at[side, part]
            )
            copy.start()
            copies.append(copy)
    for step in range(steps):
        turned[step] = matrix[me ^ step]
    rows = turned.shape[1]
    for side in range(2):
        total = None
        for part in range(traces.shape[1]):
            copies[side * traces.shape[1] + part].wait()
            left = turned[:, :, pl.ds(part * depth, depth)].reshape(steps * rows, depth)
            value = dot(left, traces[side, part])
            total = value if total is None else total + value
        total = total.astype(jnp.bfloat16)
        for step, out in enumerate(outs):
            out[pl.ds(side * rows, rows), :] = total[step * rows : (step + 1) * rows]


def spectra_call(down_traces, up_traces, matrix):
    steps, rows, depth = matrix.shape
    width = down_traces.shape[2]
    parts = 4
    return pl.pallas_call(
        functools.partial(spectra_kernel, steps),
        out_shape=(jax.ShapeDtypeStruct((2 * rows, width), jnp.bfloat16),) * steps,
        in_specs=[pl.BlockSpec(memory_space=pl.ANY)] * 2 + [pl.BlockSpec(memory_space=pltpu.VMEM)],
        out_specs=(pl.BlockSpec(memory_space=pltpu.VMEM),) * steps,
        scratch_shapes=[
            pltpu.VMEM((2, parts, depth // parts, width), jnp.bfloat16),
            pltpu.VMEM((steps, rows, depth), jnp.bfloat16),
            pltpu.SemaphoreType.DMA((2, parts)),
        ],
        compiler_params=pltpu.CompilerParams(vmem_limit_bytes=LIMIT),
        cost_estimate=pl.CostEstimate(
            flops=4 * steps * rows * depth * width, bytes_accessed=4 * depth * width, transcendentals=0
        ),
        name="spectra",
    )(down_traces.reshape(-1, width), up_traces.reshape(-1, width), matrix)


def line_shards(up_traces, down_traces):
    local_shots, samples, width = up_traces.shape
    nfreq = lax.axis_size("freq")
    core, chip = lax.axis_index("core"), lax.axis_index("chip")
    half = width // 2
    rows = width // 8
    group = 2 * local_shots
    matrix = jnp.asarray(spread_table(samples, nfreq, local_shots)).reshape(nfreq, group, -1)

    parts = spectra_call(down_traces, up_traces, matrix)
    parts = [parts[0]] + [
        lax.ppermute(parts[step], "freq", [(f, f ^ step) for f in range(nfreq)]) for step in range(1, nfreq)
    ]
    down = jnp.concatenate([part[:group] for part in parts], 0)
    up = jnp.concatenate([part[group:] for part in parts], 0)

    def inwards(array):
        return lax.ppermute(array, "chip", [(0, 1), (3, 2)])

    def across(array):
        return lax.ppermute(array, "chip", [(1, 2), (2, 1)])

    def outwards(array, turn):
        pairs = [(2 * hub + c, 2 * end + (c ^ turn)) for hub, end in ((1, 0), (2, 3)) for c in range(2)]
        return lax.ppermute(array, ("chip", "core"), pairs)

    mine = lax.dynamic_slice_in_dim(up, core * half, half, 1)
    theirs = swap_core(lax.dynamic_slice_in_dim(up, (1 - core) * half, half, 1))
    up = jnp.concatenate([mine, theirs], 0)
    chunks = [up[:, at : at + CHUNK] for at in range(0, half, CHUNK)]

    outer = inwards(down)
    inner = across(down)
    first_outer = inwards(chunks[0])
    first_inner = across(chunks[0])
    far = across(outer)
    gathered = [[chunks[0], first_outer, first_inner, across(after(first_outer, far))]]
    for chunk in chunks[1:]:
        chunk = after(chunk, outer)
        chunk_outer = inwards(chunk)
        gathered.append([chunk, chunk_outer, across(chunk), across(after(chunk_outer, gathered[-1][-1]))])

    pieces = []
    for piece in (down, outer, inner, far):
        pieces += [piece, swap_core(piece)]
    end = jnp.where(chip < 2, 0, 3)
    place = jnp.stack([2 * chip + core, 2 * chip + 1 - core, 2 * end + core, 2 * end + 1 - core]).astype(jnp.int32)
    operator = gram_call(place, pieces, local_shots, rows)
    is_end = (chip == 0) | (chip == 3)
    own, other = [], []
    for chunk in gathered:
        kept, sent, outside, crossed = solve_call(*operator, chunk)
        own.append(jnp.where(is_end, outwards(outside, 0).astype(jnp.float32), kept))
        other.append(jnp.where(is_end, outwards(crossed, 1).astype(jnp.float32), swap_core(sent)))
    own, other = jnp.concatenate(own, 2), jnp.concatenate(other, 2)
    block = jnp.where(core == 0, jnp.concatenate([own, other], 2), jnp.concatenate([other, own], 2))
    return jnp.transpose(block, (1, 0, 2))[None]


def solution(mesh):
    nfreq, nshot = mesh.devices.shape
    fine = Mesh(mesh.devices.reshape(nfreq, nshot // 2, 2), ("freq", "chip", "core"))
    spec = P(("freq", "chip", "core"), None, None)
    out_specs = P("freq", ("chip", "core"), None, None)

    def shards(up_traces, down_traces):
        shots, _, width = up_traces.shape
        line = nshot == 8 and nfreq == 4 and shots == 16 and width % (2 * CHUNK) == 0
        return (line_shards if line else ring_shards)(up_traces, down_traces)

    return jax.shard_map(shards, mesh=fine, in_specs=(spec, spec), out_specs=out_specs, check_vma=False)
```

```python
import functools
import math

import jax
import jax.numpy as jnp
import numpy as np
from jax import lax
from jax.experimental import pallas as pl
from jax.experimental.pallas import tpu as pltpu
from jax.sharding import Mesh, PartitionSpec as P

CHUNK = 256
LIMIT = 32 * 1024 * 1024
GRAM_COST = 1024
SOLVE_COST = 1024


def make_table(samples, nfreq, first):
    times = np.arange(samples)
    phase = times[:, None] * (first + np.arange(nfreq))[None, :] % samples
    angle = np.float32(2.0 * math.pi) * phase.astype(np.float32) / np.float32(samples)
    return np.stack([np.cos(angle), -np.sin(angle)], -1).astype(jnp.bfloat16)


def spread_table(samples, nfreq, shots):
    table = make_table(samples, nfreq, samples // 16).astype(np.float32)
    whole = np.einsum("tfc,sz->fcszt", table, np.eye(shots, dtype=np.float32))
    return whole.reshape(nfreq * 2 * shots, shots * samples).astype(jnp.bfloat16)


def ring_order(chips):
    return [0, 1, 3, 2] if chips == 4 else list(range(chips))


def ring_gather(piece, chips):
    order = ring_order(chips)
    pairs = [(order[i], order[(i + 1) % chips]) for i in range(chips)]
    pieces = [piece]
    for _ in range(chips - 1):
        pieces.append(lax.ppermute(pieces[-1], "chip", pairs))
    return pieces


def after(array, *others):
    return lax.optimization_barrier((array, *others))[0]


def swap_core(array):
    return lax.ppermute(array, "core", [(0, 1), (1, 0)])


def split(array):
    high = lax.reduce_precision(array, 8, 7)
    return high.astype(jnp.bfloat16), (array - high).astype(jnp.bfloat16)


def dot(left, right):
    return jnp.dot(left, right, preferred_element_type=jnp.float32)


def dot_nt(left, right):
    return lax.dot_general(left, right, (((1,), (1,)), ((), ())), preferred_element_type=jnp.float32)


def spectra(traces, matrix):
    return dot(matrix, traces.reshape(-1, traces.shape[2])).astype(jnp.bfloat16)


def to_freq(spec, nfreq):
    parts = spec.reshape(nfreq, -1, spec.shape[1])
    me = lax.axis_index("freq")
    out = []
    for step in range(nfreq):
        there = me ^ step
        part = lax.dynamic_index_in_dim(parts, there, 0, keepdims=False)
        out.append(part if step == 0 else lax.ppermute(part, "freq", [(f, f ^ step) for f in range(nfreq)]))
    return jnp.concatenate(out, 0)


def gram_kernel(shots, place, *refs):
    sources, (high, low, damping, rows_t), (both, pieces, arrived) = refs[:-7], refs[-7:-3], refs[-3:]
    count, width = sources[0].shape
    half = both.shape[0] // 2
    copies = [pltpu.make_async_copy(source, pieces.at[n], arrived.at[n]) for n, source in enumerate(sources)]
    for copy in copies:
        copy.start()
    total = jnp.zeros((1, width), jnp.float32)
    at = 0
    for number, copy in enumerate(copies):
        copy.wait()
        piece = pieces.at[number]
        for part in range(0, count, 2 * shots):
            real, imag = piece[pl.ds(part, shots), :], piece[pl.ds(part + shots, shots), :]
            both[pl.ds(at, shots), pl.ds(0, width)] = real
            both[pl.ds(at, shots), pl.ds(width, width)] = -imag
            both[pl.ds(half + at, shots), pl.ds(0, width)] = imag
            both[pl.ds(half + at, shots), pl.ds(width, width)] = real
            real, imag = real.astype(jnp.float32), imag.astype(jnp.float32)
            total += jnp.sum(real * real + imag * imag, axis=0, keepdims=True)
            at += shots
    damping[...] = 0.1 * jnp.sum(total, axis=1, keepdims=True) / width
    for at in range(0, half, 256):
        gram = dot_nt(both[pl.ds(at, 256), :], both[...])
        rounded = gram.astype(jnp.bfloat16)
        high[pl.ds(at, 256), :] = rounded
        low[pl.ds(at, 256), :] = (gram - rounded.astype(jnp.float32)).astype(jnp.bfloat16)
    wide = rows_t.shape[0] // 2
    for number in range(2):
        start = pl.multiple_of(place[number] * wide, wide)
        rows_t[pl.ds(number * wide, wide), :] = both[:, pl.ds(start, wide)].T


def gram_call(place, pieces, shots, rows):
    count, width = pieces[0].shape
    size = count * len(pieces)
    block = jax.ShapeDtypeStruct((size // 2, size), jnp.bfloat16)
    return pl.pallas_call(
        functools.partial(gram_kernel, shots),
        out_shape=(
            block,
            block,
            jax.ShapeDtypeStruct((1, 1), jnp.float32),
            jax.ShapeDtypeStruct((2 * rows, size), jnp.bfloat16),
        ),
        in_specs=[pl.BlockSpec(memory_space=pltpu.SMEM)] + [pl.BlockSpec(memory_space=pltpu.HBM)] * len(pieces),
        out_specs=(pl.BlockSpec(memory_space=pltpu.VMEM),) * 4,
        scratch_shapes=[
            pltpu.VMEM((size, 2 * width), jnp.bfloat16),
            pltpu.VMEM((len(pieces), count, width), jnp.bfloat16),
            pltpu.SemaphoreType.DMA((len(pieces),)),
        ],
        compiler_params=pltpu.CompilerParams(vmem_limit_bytes=LIMIT),
        cost_estimate=pl.CostEstimate(flops=GRAM_COST, bytes_accessed=1024, transcendentals=0),
        name="gram",
    )(place, *pieces)


def fill_turned(target, tile, value):
    half, columns = target.shape[0] // 2, target.shape[1] // 2
    target[tile, :] = value
    below = pl.ds(half + tile.start, tile.size)
    target[below, pl.ds(0, columns)] = value[:, columns:]
    target[below, pl.ds(columns, columns)] = -value[:, :columns]


def per_column(total):
    columns = total.shape[1] // 2
    total = total[:, :columns] + total[:, columns:]
    return jnp.concatenate([total, total], 1)


def two_parts(value):
    high = value.astype(jnp.bfloat16)
    return high, (value - high.astype(jnp.float32)).astype(jnp.bfloat16)


def solve_kernel(shots, first, count, damping, *refs):
    sources, refs = refs[: 3 + count], refs[3 + count :]
    block, sent, start, image, step_high, step_low, step_image, high, low, rows_t, pieces, staged, arrived = refs[-13:]
    half, columns = start.shape[0] // 2, start.shape[1] // 2
    targets = [high, low, rows_t] + [pieces.at[number] for number in range(count)]
    copies = [pltpu.make_async_copy(sources[n], target, arrived.at[n]) for n, target in enumerate(targets)]
    for copy in copies[3:] + copies[:3]:
        copy.start()
    tiles = [pl.ds(at, 256) for at in range(0, half, 256)]
    at = 0
    for number in range(count):
        copies[3 + number].wait()
        piece = pieces.at[number]
        for part in range(0, piece.shape[0], 2 * shots):
            real, imag = piece[pl.ds(part, shots), :], piece[pl.ds(part + shots, shots), :]
            fill_turned(start, pl.ds(at, shots), jnp.concatenate([real, imag], 1))
            at += shots
    copies[0].wait()
    copies[1].wait()
    damp = damping[...]
    norm_now = jnp.zeros((1, 2 * columns), jnp.float32)
    image_norm = jnp.zeros((1, 2 * columns), jnp.float32)
    for tile in tiles:
        value = dot(high[tile, :], start[...]) + dot(low[tile, :], start[...])
        image[tile, :] = value
        norm_now += jnp.sum(start[tile, :].astype(jnp.float32) * value, axis=0, keepdims=True)
        image_norm += jnp.sum(value * value, axis=0, keepdims=True)
    norm_now, image_norm = per_column(norm_now), per_column(image_norm)
    alpha = norm_now / (image_norm + damp * norm_now)
    keep = 1.0 - alpha * damp
    for tile in tiles:
        resid_high, resid_low = two_parts(keep * start[tile, :].astype(jnp.float32) - alpha * image[tile, :])
        fill_turned(step_high, tile, resid_high)
        fill_turned(step_low, tile, resid_low)
    norm_next = jnp.zeros((1, 2 * columns), jnp.float32)
    for tile in tiles:
        value = dot(high[tile, :], step_high[...]) + (
            dot(low[tile, :], step_high[...]) + dot(high[tile, :], step_low[...])
        )
        step_image[tile, :] = value
        resid = keep * start[tile, :].astype(jnp.float32) - alpha * image[tile, :]
        norm_next += jnp.sum(resid * value, axis=0, keepdims=True)
    norm_next = per_column(norm_next)
    ratio = norm_next / norm_now
    curv = jnp.zeros((1, 2 * columns), jnp.float32)
    for tile in tiles:
        direc = (keep + ratio) * start[tile, :].astype(jnp.float32) - alpha * image[tile, :]
        value = step_image[tile, :] + ratio * image[tile, :]
        curv += jnp.sum(value * (value + damp * direc), axis=0, keepdims=True)
    beta = norm_next / per_column(curv)
    from_start = alpha + beta * (keep + ratio)
    from_image = alpha * beta
    for tile in tiles:
        weight = from_start * start[tile, :].astype(jnp.float32) - from_image * image[tile, :]
        weight_high, weight_low = two_parts(weight)
        fill_turned(step_high, tile, weight_high)
        fill_turned(step_low, tile, weight_low)
    copies[2].wait()
    rows = rows_t.shape[0] // 2
    value = dot(rows_t[pl.ds(0, rows), :], step_high[...]) + dot(rows_t[pl.ds(0, rows), :], step_low[...])
    staged[:, 0, :] = value[:, :columns]
    staged[:, 1, :] = -value[:, columns:]
    offset = lax.axis_index("core") * (block.shape[2] // 2) + first
    copy = pltpu.make_async_copy(
        staged, block.at[:, :, pl.ds(pl.multiple_of(offset, columns), columns)], arrived.at[len(targets)]
    )
    copy.start()
    value = dot(rows_t[pl.ds(rows, rows), :], step_high[...]) + dot(rows_t[pl.ds(rows, rows), :], step_low[...])
    sent[...] = jnp.concatenate([value[:, :columns], -value[:, columns:]], 1)
    copy.wait()


def solve_call(high, low, damping, rows_t, pieces, shots, first, block, width):
    half, size = high.shape
    count, columns = len(pieces), pieces[0].shape[1]
    rows = rows_t.shape[0] // 2
    earlier = [] if block is None else [block]
    return pl.pallas_call(
        functools.partial(solve_kernel, shots, first, count),
        out_shape=(
            jax.ShapeDtypeStruct((rows, 2, width), jnp.float32),
            jax.ShapeDtypeStruct((rows, 2 * columns), jnp.float32),
        ),
        in_specs=[pl.BlockSpec(memory_space=pltpu.VMEM)] + [pl.BlockSpec(memory_space=pltpu.HBM)] * (3 + count + len(earlier)),
        out_specs=(pl.BlockSpec(memory_space=pltpu.HBM), pl.BlockSpec(memory_space=pltpu.VMEM)),
        input_output_aliases={4 + count: 0} if earlier else {},
        scratch_shapes=[
            pltpu.VMEM((size, 2 * columns), jnp.bfloat16),
            pltpu.VMEM((half, 2 * columns), jnp.float32),
            pltpu.VMEM((size, 2 * columns), jnp.bfloat16),
            pltpu.VMEM((size, 2 * columns), jnp.bfloat16),
            pltpu.VMEM((half, 2 * columns), jnp.float32),
            pltpu.VMEM(high.shape, jnp.bfloat16),
            pltpu.VMEM(low.shape, jnp.bfloat16),
            pltpu.VMEM(rows_t.shape, jnp.bfloat16),
            pltpu.VMEM((count,) + pieces[0].shape, jnp.bfloat16),
            pltpu.VMEM((rows, 2, columns), jnp.float32),
            pltpu.SemaphoreType.DMA((4 + count,)),
        ],
        compiler_params=pltpu.CompilerParams(vmem_limit_bytes=LIMIT),
        cost_estimate=pl.CostEstimate(flops=SOLVE_COST, bytes_accessed=1024, transcendentals=0),
        name="solve",
    )(damping, high, low, rows_t, *pieces, *earlier)


def place_kernel(_, *refs):
    sources, (block, staged, arrived) = refs[:-3], refs[-3:]
    columns = staged.shape[3]
    copies = []
    for number, source in enumerate(sources):
        staged[number, :, 0, :] = source[:, :columns]
        staged[number, :, 1, :] = source[:, columns:]
        offset = (1 - lax.axis_index("core")) * (block.shape[2] // 2) + number * columns
        copy = pltpu.make_async_copy(
            staged.at[number], block.at[:, :, pl.ds(pl.multiple_of(offset, columns), columns)], arrived.at[number]
        )
        copy.start()
        copies.append(copy)
    for copy in copies:
        copy.wait()


def place_call(block, got):
    rows, columns = got[0].shape
    return pl.pallas_call(
        place_kernel,
        out_shape=jax.ShapeDtypeStruct(block.shape, jnp.float32),
        in_specs=[pl.BlockSpec(memory_space=pltpu.HBM)] + [pl.BlockSpec(memory_space=pltpu.VMEM)] * len(got),
        out_specs=pl.BlockSpec(memory_space=pltpu.HBM),
        input_output_aliases={0: 0},
        scratch_shapes=[
            pltpu.VMEM((len(got), rows, 2, columns // 2), jnp.float32),
            pltpu.SemaphoreType.DMA((len(got),)),
        ],
        compiler_params=pltpu.CompilerParams(vmem_limit_bytes=LIMIT),
        name="place",
    )(block, *got)


def plain_gram(place, pieces, shots, rows):
    width = pieces[0].shape[1]
    even = jnp.concatenate(pieces, 0)
    turned = even.reshape(-1, 2, shots, width)
    odd = jnp.stack([-turned[:, 1], turned[:, 0]], 1).reshape(even.shape)
    blocks = []
    for number in range(2):
        blocks.append(lax.dynamic_slice_in_dim(even, place[number] * rows, rows, 1).T)
        blocks.append(-lax.dynamic_slice_in_dim(odd, place[number] * rows, rows, 1).T)
    return even, odd, 0.1 * jnp.sum(jnp.square(even.astype(jnp.float32))) / width, jnp.concatenate(blocks, 0)


def dot_tn(left, right):
    return lax.dot_general(left, right, (((0,), (0,)), ((), ())), preferred_element_type=jnp.float32)


def plain_apply(even, odd, parts):
    out = []
    for side in (even, odd):
        high, low = split(sum(dot_tn(side, part) for part in parts))
        out.append(dot(side, high) + dot(side, low))
    return out[0] + out[1]


def plain_solve(even, odd, damping, rows_t, pieces):
    start = jnp.concatenate(pieces, 0)
    wide = start.astype(jnp.float32)
    image = plain_apply(even, odd, (start,))
    norm_now = jnp.sum(wide * image, axis=0)
    alpha = norm_now / (jnp.sum(image * image, axis=0) + damping * norm_now)
    resid = (1.0 - alpha * damping) * wide - alpha * image
    resid_image = plain_apply(even, odd, split(resid))
    norm_next = jnp.sum(resid * resid_image, axis=0)
    ratio = norm_next / norm_now
    direc = resid + ratio * wide
    direc_image = resid_image + ratio * image
    curv = jnp.sum(direc_image * (direc_image + damping * direc), axis=0)
    weights_high, weights_low = split(alpha * wide + norm_next / curv * direc)
    block = (dot(rows_t, weights_high) + dot(rows_t, weights_low)).reshape(2, 2, -1, start.shape[1])
    return block[0], block[1]


def shards(up_traces, down_traces):
    local_shots, samples, width = up_traces.shape
    nfreq, chips = lax.axis_size("freq"), lax.axis_size("chip")
    core = lax.axis_index("core")
    half = width // 2
    rows = width // (2 * chips)
    size = 2 * local_shots * nfreq * 2 * chips
    matrix = jnp.asarray(spread_table(samples, nfreq, local_shots))

    down_spec = spectra(down_traces, matrix)
    up_spec = spectra(up_traces, after(matrix, down_spec))
    down = after(to_freq(down_spec, nfreq), up_spec)
    own = ring_gather(down, chips)

    up = to_freq(after(up_spec, down), nfreq)
    mine = lax.dynamic_slice_in_dim(up, core * half, half, 1)
    theirs = swap_core(lax.dynamic_slice_in_dim(up, (1 - core) * half, half, 1))
    up = jnp.concatenate([mine, theirs], 0)

    pieces = []
    for piece in own:
        pieces += [piece, swap_core(piece)]
    place = 2 * lax.axis_index("chip") + jnp.stack([core, 1 - core]).astype(jnp.int32)

    small = 2 * chips * 2 * local_shots * nfreq <= 1024 and rows == 128 and half == 2 * CHUNK and local_shots == 16
    if not small:
        operator = plain_gram(place, pieces, local_shots, rows)
        chunk = CHUNK if half % CHUNK == 0 else half
        kept, got = [], []
        for at in range(0, half, chunk):
            stay, send = plain_solve(*operator, ring_gather(up[:, at : at + chunk], chips))
            kept.append(stay)
            got.append(swap_core(send))
        kept, got = jnp.concatenate(kept, 2), jnp.concatenate(got, 2)
        first = core == 0
        block = jnp.concatenate([jnp.where(first, kept, got), jnp.where(first, got, kept)], 2)
        return jnp.transpose(block, (1, 0, 2))[None]

    early = ring_gather(up[:, :CHUNK], chips)
    late = ring_gather(after(up[:, CHUNK:], own[2]), chips)
    place = after(place, late[1])
    operator = gram_call(place, pieces, local_shots, rows)
    early[0] = after(early[0], late[2])
    block, sent_early = solve_call(*operator, early, local_shots, 0, None, width)
    block, sent_late = solve_call(*operator, late, local_shots, CHUNK, block, width)
    return place_call(block, [swap_core(sent_early), swap_core(sent_late)])[None]


def solution(mesh):
    nfreq, nshot = mesh.devices.shape
    fine = Mesh(mesh.devices.reshape(nfreq, nshot // 2, 2), ("freq", "chip", "core"))
    spec = P(("freq", "chip", "core"), None, None)
    out_specs = P("freq", ("chip", "core"), None, None)
    return jax.shard_map(shards, mesh=fine, in_specs=(spec, spec), out_specs=out_specs, check_vma=False)
```

```python
import functools
import math

import jax
import jax.numpy as jnp
import numpy as np
from jax import lax
from jax.experimental import pallas as pl
from jax.experimental.pallas import tpu as pltpu
from jax.sharding import Mesh, PartitionSpec as P

CHUNK = 256
LIMIT = 32 * 1024 * 1024
GRAM_COST = 20_000_000_000
SOLVE_COST = 1024


def make_table(samples, nfreq, first):
    times = np.arange(samples)
    phase = times[:, None] * (first + np.arange(nfreq))[None, :] % samples
    angle = np.float32(2.0 * math.pi) * phase.astype(np.float32) / np.float32(samples)
    return np.stack([np.cos(angle), -np.sin(angle)], -1).astype(jnp.bfloat16)


def spread_table(samples, nfreq, shots):
    table = make_table(samples, nfreq, samples // 16).astype(np.float32)
    whole = np.einsum("tfc,sz->fcszt", table, np.eye(shots, dtype=np.float32))
    return whole.reshape(nfreq * 2 * shots, shots * samples).astype(jnp.bfloat16)


def ring_order(chips):
    return [0, 1, 3, 2] if chips == 4 else list(range(chips))


def ring_gather(piece, chips):
    order = ring_order(chips)
    pairs = [(order[i], order[(i + 1) % chips]) for i in range(chips)]
    pieces = [piece]
    for _ in range(chips - 1):
        pieces.append(lax.ppermute(pieces[-1], "chip", pairs))
    return pieces


def after(array, *others):
    return lax.optimization_barrier((array, *others))[0]


def swap_core(array):
    return lax.ppermute(array, "core", [(0, 1), (1, 0)])


def split(array):
    high = lax.reduce_precision(array, 8, 7)
    return high.astype(jnp.bfloat16), (array - high).astype(jnp.bfloat16)


def dot(left, right):
    return jnp.dot(left, right, preferred_element_type=jnp.float32)


def dot_nt(left, right):
    return lax.dot_general(left, right, (((1,), (1,)), ((), ())), preferred_element_type=jnp.float32)


def spectra(traces, matrix):
    return dot(matrix, traces.reshape(-1, traces.shape[2])).astype(jnp.bfloat16)


def to_freq(spec, nfreq):
    parts = spec.reshape(nfreq, -1, spec.shape[1])
    me = lax.axis_index("freq")
    out = []
    for step in range(nfreq):
        there = me ^ step
        part = lax.dynamic_index_in_dim(parts, there, 0, keepdims=False)
        out.append(part if step == 0 else lax.ppermute(part, "freq", [(f, f ^ step) for f in range(nfreq)]))
    return jnp.concatenate(out, 0)


def gram_kernel(shots, place, *refs):
    sources, (high, low, damping, rows_t), (both, pieces, arrived) = refs[:-7], refs[-7:-3], refs[-3:]
    count, width = sources[0].shape
    half = both.shape[0] // 2
    copies = [pltpu.make_async_copy(source, pieces.at[n], arrived.at[n]) for n, source in enumerate(sources)]
    for copy in copies:
        copy.start()
    total = jnp.zeros((1, width), jnp.float32)
    at = 0
    for number, copy in enumerate(copies):
        copy.wait()
        piece = pieces.at[number]
        for part in range(0, count, 2 * shots):
            real, imag = piece[pl.ds(part, shots), :], piece[pl.ds(part + shots, shots), :]
            both[pl.ds(at, shots), pl.ds(0, width)] = real
            both[pl.ds(at, shots), pl.ds(width, width)] = -imag
            both[pl.ds(half + at, shots), pl.ds(0, width)] = imag
            both[pl.ds(half + at, shots), pl.ds(width, width)] = real
            real, imag = real.astype(jnp.float32), imag.astype(jnp.float32)
            total += jnp.sum(real * real + imag * imag, axis=0, keepdims=True)
            at += shots
    damping[...] = 0.1 * jnp.sum(total, axis=1, keepdims=True) / width
    for at in range(0, half, 256):
        gram = dot_nt(both[pl.ds(at, 256), :], both[...])
        rounded = gram.astype(jnp.bfloat16)
        high[pl.ds(at, 256), :] = rounded
        low[pl.ds(at, 256), :] = (gram - rounded.astype(jnp.float32)).astype(jnp.bfloat16)
    wide = rows_t.shape[0] // 2
    for number in range(2):
        start = pl.multiple_of(place[number] * wide, wide)
        rows_t[pl.ds(number * wide, wide), :] = both[:, pl.ds(start, wide)].T


def gram_call(place, pieces, shots, rows):
    count, width = pieces[0].shape
    size = count * len(pieces)
    block = jax.ShapeDtypeStruct((size // 2, size), jnp.bfloat16)
    return pl.pallas_call(
        functools.partial(gram_kernel, shots),
        out_shape=(
            block,
            block,
            jax.ShapeDtypeStruct((1, 1), jnp.float32),
            jax.ShapeDtypeStruct((2 * rows, size), jnp.bfloat16),
        ),
        in_specs=[pl.BlockSpec(memory_space=pltpu.SMEM)] + [pl.BlockSpec(memory_space=pltpu.HBM)] * len(pieces),
        out_specs=(pl.BlockSpec(memory_space=pltpu.VMEM),) * 4,
        scratch_shapes=[
            pltpu.VMEM((size, 2 * width), jnp.bfloat16),
            pltpu.VMEM((len(pieces), count, width), jnp.bfloat16),
            pltpu.SemaphoreType.DMA((len(pieces),)),
        ],
        compiler_params=pltpu.CompilerParams(vmem_limit_bytes=LIMIT),
        cost_estimate=pl.CostEstimate(flops=GRAM_COST, bytes_accessed=1024, transcendentals=0),
        name="gram",
    )(place, *pieces)


def fill_turned(target, tile, value):
    half, columns = target.shape[0] // 2, target.shape[1] // 2
    target[tile, :] = value
    below = pl.ds(half + tile.start, tile.size)
    target[below, pl.ds(0, columns)] = value[:, columns:]
    target[below, pl.ds(columns, columns)] = -value[:, :columns]


def per_column(total):
    columns = total.shape[1] // 2
    total = total[:, :columns] + total[:, columns:]
    return jnp.concatenate([total, total], 1)


def two_parts(value):
    high = value.astype(jnp.bfloat16)
    return high, (value - high.astype(jnp.float32)).astype(jnp.bfloat16)


def solve_kernel(shots, first, count, damping, *refs):
    high, low, rows_t, sources = refs[0], refs[1], refs[2], refs[3 : 3 + count]
    block, sent, start, image, step_high, step_low, step_image, pieces, staged, arrived = refs[-10:]
    half, columns = start.shape[0] // 2, start.shape[1] // 2
    copies = [pltpu.make_async_copy(source, pieces.at[n], arrived.at[n]) for n, source in enumerate(sources)]
    for copy in copies:
        copy.start()
    tiles = [pl.ds(at, 256) for at in range(0, half, 256)]
    at = 0
    for number in range(count):
        copies[number].wait()
        piece = pieces.at[number]
        for part in range(0, piece.shape[0], 2 * shots):
            real, imag = piece[pl.ds(part, shots), :], piece[pl.ds(part + shots, shots), :]
            fill_turned(start, pl.ds(at, shots), jnp.concatenate([real, imag], 1))
            at += shots
    damp = damping[...]
    norm_now = jnp.zeros((1, 2 * columns), jnp.float32)
    image_norm = jnp.zeros((1, 2 * columns), jnp.float32)
    for tile in tiles:
        value = dot(high[tile, :], start[...]) + dot(low[tile, :], start[...])
        image[tile, :] = value
        norm_now += jnp.sum(start[tile, :].astype(jnp.float32) * value, axis=0, keepdims=True)
        image_norm += jnp.sum(value * value, axis=0, keepdims=True)
    norm_now, image_norm = per_column(norm_now), per_column(image_norm)
    alpha = norm_now / (image_norm + damp * norm_now)
    keep = 1.0 - alpha * damp
    for tile in tiles:
        resid_high, resid_low = two_parts(keep * start[tile, :].astype(jnp.float32) - alpha * image[tile, :])
        fill_turned(step_high, tile, resid_high)
        fill_turned(step_low, tile, resid_low)
    norm_next = jnp.zeros((1, 2 * columns), jnp.float32)
    for tile in tiles:
        value = dot(high[tile, :], step_high[...]) + (
            dot(low[tile, :], step_high[...]) + dot(high[tile, :], step_low[...])
        )
        step_image[tile, :] = value
        resid = keep * start[tile, :].astype(jnp.float32) - alpha * image[tile, :]
        norm_next += jnp.sum(resid * value, axis=0, keepdims=True)
    norm_next = per_column(norm_next)
    ratio = norm_next / norm_now
    curv = jnp.zeros((1, 2 * columns), jnp.float32)
    for tile in tiles:
        direc = (keep + ratio) * start[tile, :].astype(jnp.float32) - alpha * image[tile, :]
        value = step_image[tile, :] + ratio * image[tile, :]
        curv += jnp.sum(value * (value + damp * direc), axis=0, keepdims=True)
    beta = norm_next / per_column(curv)
    from_start = alpha + beta * (keep + ratio)
    from_image = alpha * beta
    for tile in tiles:
        weight = from_start * start[tile, :].astype(jnp.float32) - from_image * image[tile, :]
        weight_high, weight_low = two_parts(weight)
        fill_turned(step_high, tile, weight_high)
        fill_turned(step_low, tile, weight_low)
    rows = rows_t.shape[0] // 2
    value = dot(rows_t[pl.ds(0, rows), :], step_high[...]) + dot(rows_t[pl.ds(0, rows), :], step_low[...])
    staged[:, 0, :] = value[:, :columns]
    staged[:, 1, :] = -value[:, columns:]
    offset = lax.axis_index("core") * (block.shape[2] // 2) + first
    copy = pltpu.make_async_copy(
        staged, block.at[:, :, pl.ds(pl.multiple_of(offset, columns), columns)], arrived.at[count]
    )
    copy.start()
    value = dot(rows_t[pl.ds(rows, rows), :], step_high[...]) + dot(rows_t[pl.ds(rows, rows), :], step_low[...])
    sent[...] = jnp.concatenate([value[:, :columns], -value[:, columns:]], 1)
    copy.wait()


def solve_call(high, low, damping, rows_t, pieces, shots, first, block, width):
    half, size = high.shape
    count, columns = len(pieces), pieces[0].shape[1]
    rows = rows_t.shape[0] // 2
    earlier = [] if block is None else [block]
    return pl.pallas_call(
        functools.partial(solve_kernel, shots, first, count),
        out_shape=(
            jax.ShapeDtypeStruct((rows, 2, width), jnp.float32),
            jax.ShapeDtypeStruct((rows, 2 * columns), jnp.float32),
        ),
        in_specs=[pl.BlockSpec(memory_space=pltpu.VMEM)] * 4
        + [pl.BlockSpec(memory_space=pltpu.HBM)] * (count + len(earlier)),
        out_specs=(pl.BlockSpec(memory_space=pltpu.HBM), pl.BlockSpec(memory_space=pltpu.VMEM)),
        input_output_aliases={4 + count: 0} if earlier else {},
        scratch_shapes=[
            pltpu.VMEM((size, 2 * columns), jnp.bfloat16),
            pltpu.VMEM((half, 2 * columns), jnp.float32),
            pltpu.VMEM((size, 2 * columns), jnp.bfloat16),
            pltpu.VMEM((size, 2 * columns), jnp.bfloat16),
            pltpu.VMEM((half, 2 * columns), jnp.float32),
            pltpu.VMEM((count,) + pieces[0].shape, jnp.bfloat16),
            pltpu.VMEM((rows, 2, columns), jnp.float32),
            pltpu.SemaphoreType.DMA((1 + count,)),
        ],
        compiler_params=pltpu.CompilerParams(vmem_limit_bytes=LIMIT),
        cost_estimate=pl.CostEstimate(flops=SOLVE_COST, bytes_accessed=1024, transcendentals=0),
        name="solve",
    )(damping, high, low, rows_t, *pieces, *earlier)


def place_kernel(_, *refs):
    sources, (block, staged, arrived) = refs[:-3], refs[-3:]
    columns = staged.shape[3]
    copies = []
    for number, source in enumerate(sources):
        staged[number, :, 0, :] = source[:, :columns]
        staged[number, :, 1, :] = source[:, columns:]
        offset = (1 - lax.axis_index("core")) * (block.shape[2] // 2) + number * columns
        copy = pltpu.make_async_copy(
            staged.at[number], block.at[:, :, pl.ds(pl.multiple_of(offset, columns), columns)], arrived.at[number]
        )
        copy.start()
        copies.append(copy)
    for copy in copies:
        copy.wait()


def place_call(block, got):
    rows, columns = got[0].shape
    return pl.pallas_call(
        place_kernel,
        out_shape=jax.ShapeDtypeStruct(block.shape, jnp.float32),
        in_specs=[pl.BlockSpec(memory_space=pltpu.HBM)] + [pl.BlockSpec(memory_space=pltpu.VMEM)] * len(got),
        out_specs=pl.BlockSpec(memory_space=pltpu.HBM),
        input_output_aliases={0: 0},
        scratch_shapes=[
            pltpu.VMEM((len(got), rows, 2, columns // 2), jnp.float32),
            pltpu.SemaphoreType.DMA((len(got),)),
        ],
        compiler_params=pltpu.CompilerParams(vmem_limit_bytes=LIMIT),
        name="place",
    )(block, *got)


def plain_gram(place, pieces, shots, rows):
    width = pieces[0].shape[1]
    even = jnp.concatenate(pieces, 0)
    turned = even.reshape(-1, 2, shots, width)
    odd = jnp.stack([-turned[:, 1], turned[:, 0]], 1).reshape(even.shape)
    blocks = []
    for number in range(2):
        blocks.append(lax.dynamic_slice_in_dim(even, place[number] * rows, rows, 1).T)
        blocks.append(-lax.dynamic_slice_in_dim(odd, place[number] * rows, rows, 1).T)
    return even, odd, 0.1 * jnp.sum(jnp.square(even.astype(jnp.float32))) / width, jnp.concatenate(blocks, 0)


def dot_tn(left, right):
    return lax.dot_general(left, right, (((0,), (0,)), ((), ())), preferred_element_type=jnp.float32)


def plain_apply(even, odd, parts):
    out = []
    for side in (even, odd):
        high, low = split(sum(dot_tn(side, part) for part in parts))
        out.append(dot(side, high) + dot(side, low))
    return out[0] + out[1]


def plain_solve(even, odd, damping, rows_t, pieces):
    start = jnp.concatenate(pieces, 0)
    wide = start.astype(jnp.float32)
    image = plain_apply(even, odd, (start,))
    norm_now = jnp.sum(wide * image, axis=0)
    alpha = norm_now / (jnp.sum(image * image, axis=0) + damping * norm_now)
    resid = (1.0 - alpha * damping) * wide - alpha * image
    resid_image = plain_apply(even, odd, split(resid))
    norm_next = jnp.sum(resid * resid_image, axis=0)
    ratio = norm_next / norm_now
    direc = resid + ratio * wide
    direc_image = resid_image + ratio * image
    curv = jnp.sum(direc_image * (direc_image + damping * direc), axis=0)
    weights_high, weights_low = split(alpha * wide + norm_next / curv * direc)
    block = (dot(rows_t, weights_high) + dot(rows_t, weights_low)).reshape(2, 2, -1, start.shape[1])
    return block[0], block[1]


def shards(up_traces, down_traces):
    local_shots, samples, width = up_traces.shape
    nfreq, chips = lax.axis_size("freq"), lax.axis_size("chip")
    core = lax.axis_index("core")
    half = width // 2
    rows = width // (2 * chips)
    size = 2 * local_shots * nfreq * 2 * chips
    matrix = jnp.asarray(spread_table(samples, nfreq, local_shots))

    down_spec = spectra(down_traces, matrix)
    up_spec = spectra(up_traces, after(matrix, down_spec))
    down = after(to_freq(down_spec, nfreq), up_spec)
    own = ring_gather(down, chips)

    up = to_freq(after(up_spec, down), nfreq)
    mine = lax.dynamic_slice_in_dim(up, core * half, half, 1)
    theirs = swap_core(lax.dynamic_slice_in_dim(up, (1 - core) * half, half, 1))
    up = jnp.concatenate([mine, theirs], 0)

    pieces = []
    for piece in own:
        pieces += [piece, swap_core(piece)]
    place = 2 * lax.axis_index("chip") + jnp.stack([core, 1 - core]).astype(jnp.int32)

    small = 2 * chips * 2 * local_shots * nfreq <= 1024 and rows == 128 and half == 2 * CHUNK and local_shots == 16
    if not small:
        operator = plain_gram(place, pieces, local_shots, rows)
        chunk = CHUNK if half % CHUNK == 0 else half
        kept, got = [], []
        for at in range(0, half, chunk):
            stay, send = plain_solve(*operator, ring_gather(up[:, at : at + chunk], chips))
            kept.append(stay)
            got.append(swap_core(send))
        kept, got = jnp.concatenate(kept, 2), jnp.concatenate(got, 2)
        first = core == 0
        block = jnp.concatenate([jnp.where(first, kept, got), jnp.where(first, got, kept)], 2)
        return jnp.transpose(block, (1, 0, 2))[None]

    gathered = ring_gather(up, chips)
    operator = gram_call(place, pieces, local_shots, rows)
    block, sent = solve_call(*operator, gathered, local_shots, 0, None, width)
    return place_call(block, [swap_core(sent)])[None]


def solution(mesh):
    nfreq, nshot = mesh.devices.shape
    fine = Mesh(mesh.devices.reshape(nfreq, nshot // 2, 2), ("freq", "chip", "core"))
    spec = P(("freq", "chip", "core"), None, None)
    out_specs = P("freq", ("chip", "core"), None, None)
    return jax.shard_map(shards, mesh=fine, in_specs=(spec, spec), out_specs=out_specs, check_vma=False)
```

```python
import functools
import math

import jax
import jax.numpy as jnp
import numpy as np
from jax import lax
from jax.experimental import pallas as pl
from jax.experimental.pallas import tpu as pltpu
from jax.sharding import Mesh, PartitionSpec as P

CHUNK = 256
LIMIT = 32 * 1024 * 1024
GRAM_COST = 1024
SOLVE_COST = 1024
KEEP_COST = 1_000_000_000
STAGE_COST = 1024


def make_table(samples, nfreq, first):
    times = np.arange(samples)
    phase = times[:, None] * (first + np.arange(nfreq))[None, :] % samples
    angle = np.float32(2.0 * math.pi) * phase.astype(np.float32) / np.float32(samples)
    return np.stack([np.cos(angle), -np.sin(angle)], -1).astype(jnp.bfloat16)


def spread_table(samples, nfreq, shots):
    table = make_table(samples, nfreq, samples // 16).astype(np.float32)
    whole = np.einsum("tfc,sz->fcszt", table, np.eye(shots, dtype=np.float32))
    return whole.reshape(nfreq * 2 * shots, shots * samples).astype(jnp.bfloat16)


def ring_order(chips):
    return [0, 1, 3, 2] if chips == 4 else list(range(chips))


def ring_gather(piece, chips, *before_last):
    order = ring_order(chips)
    pairs = [(order[i], order[(i + 1) % chips]) for i in range(chips)]
    pieces = [piece]
    for step in range(1, chips):
        piece = after(pieces[-1], *before_last) if step == chips - 1 and before_last else pieces[-1]
        pieces.append(lax.ppermute(piece, "chip", pairs))
    return pieces


def after(array, *others):
    return lax.optimization_barrier((array, *others))[0]


def swap_core(array):
    return lax.ppermute(array, "core", [(0, 1), (1, 0)])


def split(array):
    high = lax.reduce_precision(array, 8, 7)
    return high.astype(jnp.bfloat16), (array - high).astype(jnp.bfloat16)


def dot(left, right):
    return jnp.dot(left, right, preferred_element_type=jnp.float32)


def dot_nt(left, right):
    return lax.dot_general(left, right, (((1,), (1,)), ((), ())), preferred_element_type=jnp.float32)


def spectra(traces, matrix):
    return dot(matrix, traces.reshape(-1, traces.shape[2])).astype(jnp.bfloat16)


def to_freq(spec, nfreq):
    parts = spec.reshape(nfreq, -1, spec.shape[1])
    me = lax.axis_index("freq")
    out = []
    for step in range(nfreq):
        there = me ^ step
        part = lax.dynamic_index_in_dim(parts, there, 0, keepdims=False)
        out.append(part if step == 0 else lax.ppermute(part, "freq", [(f, f ^ step) for f in range(nfreq)]))
    return jnp.concatenate(out, 0)


def gram_kernel(shots, place, *refs):
    pieces, (high, low, damping, rows_t), both = refs[:-5], refs[-5:-1], refs[-1]
    count, width = pieces[0].shape
    total = jnp.zeros((1, width), jnp.float32)
    for number, piece in enumerate(pieces):
        at = number // 2 * 2 * count + number % 2 * (count // 2)
        for part in range(0, count, 2 * shots):
            real, imag = piece[pl.ds(part, shots), :], piece[pl.ds(part + shots, shots), :]
            both[pl.ds(at, shots), pl.ds(0, width)] = real
            both[pl.ds(at, shots), pl.ds(width, width)] = -imag
            both[pl.ds(count + at, shots), pl.ds(0, width)] = imag
            both[pl.ds(count + at, shots), pl.ds(width, width)] = real
            real, imag = real.astype(jnp.float32), imag.astype(jnp.float32)
            total += jnp.sum(real * real + imag * imag, axis=0, keepdims=True)
            at += shots
    damping[...] = 0.1 * jnp.sum(total, axis=1, keepdims=True) / width
    left = jnp.concatenate([both[pl.ds(at, count), :] for at in range(0, both.shape[0], 2 * count)], 0)
    for at in range(0, left.shape[0], 256):
        gram = dot_nt(left[at : at + 256], both[...])
        rounded = gram.astype(jnp.bfloat16)
        high[pl.ds(at, 256), :] = rounded
        low[pl.ds(at, 256), :] = (gram - rounded.astype(jnp.float32)).astype(jnp.bfloat16)
    wide = rows_t.shape[0] // 2
    for number in range(2):
        start = pl.multiple_of(place[number] * wide, wide)
        rows_t[pl.ds(number * wide, wide), :] = both[:, pl.ds(start, wide)].T


def gram_call(place, pieces, shots, rows):
    count, width = pieces[0].shape
    size = count * len(pieces)
    block = jax.ShapeDtypeStruct((size // 2, size), jnp.bfloat16)
    return pl.pallas_call(
        functools.partial(gram_kernel, shots),
        out_shape=(
            block,
            block,
            jax.ShapeDtypeStruct((1, 1), jnp.float32),
            jax.ShapeDtypeStruct((2 * rows, size), jnp.bfloat16),
        ),
        in_specs=[pl.BlockSpec(memory_space=pltpu.SMEM)] + [pl.BlockSpec(memory_space=pltpu.VMEM)] * len(pieces),
        out_specs=(pl.BlockSpec(memory_space=pltpu.VMEM),) * 4,
        scratch_shapes=[pltpu.VMEM((size, 2 * width), jnp.bfloat16)],
        compiler_params=pltpu.CompilerParams(vmem_limit_bytes=LIMIT),
        cost_estimate=pl.CostEstimate(flops=GRAM_COST, bytes_accessed=1024, transcendentals=0),
        name="gram",
    )(place, *pieces)


def fill_turned(target, at, below, value):
    count, columns = value.shape[0], value.shape[1] // 2
    target[pl.ds(at, count), :] = value
    target[pl.ds(below, count), pl.ds(0, columns)] = value[:, columns:]
    target[pl.ds(below, count), pl.ds(columns, columns)] = -value[:, :columns]


def fill_piece(shots, source, first, target, number):
    count, columns = source.shape[0], target.shape[1] // 2
    at = number * count
    for part in range(0, count, 2 * shots):
        real, imag = (source[pl.ds(part + side, shots), pl.ds(first, columns)] for side in (0, shots))
        fill_turned(target, at, at + count // 2, jnp.concatenate([real, imag], 1))
        at += shots


def per_column(total):
    columns = total.shape[1] // 2
    total = total[:, :columns] + total[:, columns:]
    return jnp.concatenate([total, total], 1)


def two_parts(value):
    high = value.astype(jnp.bfloat16)
    return high, (value - high.astype(jnp.float32)).astype(jnp.bfloat16)


def taking_turns(*lists):
    for number in range(max(len(steps) for steps in lists)):
        for steps in lists:
            if number < len(steps):
                steps[number]()


class Half:
    def __init__(self, high, low, damping, early, earlier, late, image, step_high, step_low, step_image):
        self.high, self.low, self.damping = high, low, damping
        self.early, self.earlier, self.late, self.image = early, earlier, late, image
        self.step_high, self.step_low, self.step_image = step_high, step_low, step_image
        self.count, self.columns = late.shape[0] // 2, late.shape[1] // 2
        self.blocks = range(high.shape[0] // self.count)
        self.sums = [jnp.zeros((1, 2 * self.columns), jnp.float32) for _ in range(4)]

    def rows(self, block):
        return pl.ds(block * self.count, self.count)

    def add(self, which, value):
        self.sums[which] = self.sums[which] + jnp.sum(value, axis=0, keepdims=True)

    def begin(self, block):
        last = block == self.blocks[-1]
        ref, at = (self.late, 0) if last else (self.early, 2 * block * self.count)
        return ref[pl.ds(at, self.count), :].astype(jnp.float32)

    def resid(self, block):
        return self.keep * self.begin(block) - self.alpha * self.image[self.rows(block), :]

    def store(self, block, value):
        at = 2 * block * self.count
        for target, part in zip((self.step_high, self.step_low), two_parts(value)):
            fill_turned(target, at, at + self.count, part)

    def apply_start(self):
        columns = pl.ds(self.early.shape[0], 2 * self.count)

        def step(block):
            rows = self.rows(block)
            value = self.earlier[rows, :] + (
                dot(self.high[rows, columns], self.late[...]) + dot(self.low[rows, columns], self.late[...])
            )
            self.image[rows, :] = value
            self.add(0, self.begin(block) * value)
            self.add(1, value * value)

        return [functools.partial(step, block) for block in self.blocks]

    def take_step(self):
        def scalars():
            self.norm_now, image_norm = per_column(self.sums[0]), per_column(self.sums[1])
            self.alpha = self.norm_now / (image_norm + self.damping * self.norm_now)
            self.keep = 1.0 - self.alpha * self.damping

        def step(block):
            self.store(block, self.resid(block))

        return [scalars] + [functools.partial(step, block) for block in self.blocks]

    def apply_step(self):
        def step(block):
            rows = self.rows(block)
            value = dot(self.high[rows, :], self.step_high[...]) + (
                dot(self.low[rows, :], self.step_high[...]) + dot(self.high[rows, :], self.step_low[...])
            )
            self.step_image[rows, :] = value
            self.add(2, self.resid(block) * value)

        return [functools.partial(step, block) for block in self.blocks]

    def weigh(self):
        def scalars():
            self.norm_next = per_column(self.sums[2])
            self.ratio = self.norm_next / self.norm_now

        def curvature(block):
            rows = self.rows(block)
            direc = self.resid(block) + self.ratio * self.begin(block)
            value = self.step_image[rows, :] + self.ratio * self.image[rows, :]
            self.add(3, value * (value + self.damping * direc))

        def more_scalars():
            beta = self.norm_next / per_column(self.sums[3])
            self.from_start = self.alpha + beta * (self.keep + self.ratio)
            self.from_image = self.alpha * beta

        def step(block):
            self.store(block, self.from_start * self.begin(block) - self.from_image * self.image[self.rows(block), :])

        return (
            [scalars]
            + [functools.partial(curvature, block) for block in self.blocks]
            + [more_scalars]
            + [functools.partial(step, block) for block in self.blocks]
        )


def stage_kernel(shots, high, low, *refs):
    sources, (early, earlier) = refs[:-2], refs[-2:]
    columns, known = early.shape[2] // 2, pl.ds(0, early.shape[1])
    for h in range(2):
        for number, source in enumerate(sources):
            fill_piece(shots, source, h * columns, early.at[h], number)
    for h in range(2):
        for at in range(0, high.shape[0], 128):
            rows = pl.ds(at, 128)
            earlier[h, rows, :] = dot(high[rows, known], early[h]) + dot(low[rows, known], early[h])


def stage_call(high, low, pieces, shots):
    half = high.shape[0]
    rows, columns = pieces[0].shape
    return pl.pallas_call(
        functools.partial(stage_kernel, shots),
        out_shape=(
            jax.ShapeDtypeStruct((2, len(pieces) * rows, columns), jnp.bfloat16),
            jax.ShapeDtypeStruct((2, half, columns), jnp.float32),
        ),
        in_specs=[pl.BlockSpec(memory_space=pltpu.VMEM)] * (2 + len(pieces)),
        out_specs=(pl.BlockSpec(memory_space=pltpu.VMEM),) * 2,
        compiler_params=pltpu.CompilerParams(vmem_limit_bytes=LIMIT),
        cost_estimate=pl.CostEstimate(flops=STAGE_COST, bytes_accessed=1024, transcendentals=0),
        name="stage",
    )(high, low, *pieces)


def solve_kernel(
    shots, high, low, damping, rows_t, early, earlier, piece, sent, weights_high, weights_low, late, image, step_image
):
    columns = late.shape[2] // 2
    damp = damping[...]
    one, two = (
        Half(
            high, low, damp, *(ref.at[h] for ref in (early, earlier, late, image, weights_high, weights_low, step_image))
        )
        for h in range(2)
    )
    rows = rows_t.shape[0] // 2

    def project(h):
        def step():
            left = rows_t[pl.ds(rows, rows), :]
            value = dot(left, weights_high[h]) + dot(left, weights_low[h])
            sent[:, pl.ds(h * columns, columns)] = value[:, :columns]
            sent[:, pl.ds((2 + h) * columns, columns)] = -value[:, columns:]

        return [step]

    fill_piece(shots, piece, 0, late.at[0], 0)
    fill_piece(shots, piece, columns, late.at[1], 0)
    taking_turns(one.apply_start())
    taking_turns(two.apply_start(), one.take_step())
    taking_turns(one.apply_step(), two.take_step())
    taking_turns(two.apply_step(), one.weigh())
    taking_turns(project(0), two.weigh())
    taking_turns(project(1))


def solve_call(high, low, damping, rows_t, early, earlier, piece, shots):
    half, size = high.shape
    count, columns = piece.shape[0], piece.shape[1] // 2
    rows = rows_t.shape[0] // 2
    weights = jax.ShapeDtypeStruct((2, size, 2 * columns), jnp.bfloat16)
    return pl.pallas_call(
        functools.partial(solve_kernel, shots),
        out_shape=(jax.ShapeDtypeStruct((rows, 4 * columns), jnp.float32), weights, weights),
        in_specs=[pl.BlockSpec(memory_space=pltpu.VMEM)] * 7,
        out_specs=(pl.BlockSpec(memory_space=pltpu.VMEM),) * 3,
        scratch_shapes=[
            pltpu.VMEM((2, count, 2 * columns), jnp.bfloat16),
            pltpu.VMEM((2, half, 2 * columns), jnp.float32),
            pltpu.VMEM((2, half, 2 * columns), jnp.float32),
        ],
        compiler_params=pltpu.CompilerParams(vmem_limit_bytes=LIMIT),
        cost_estimate=pl.CostEstimate(flops=SOLVE_COST, bytes_accessed=1024, transcendentals=0),
        name="solve",
    )(high, low, damping, rows_t, early, earlier, piece)


def keep_kernel(rows_t, weights_high, weights_low, block, staged, arrived):
    rows, columns = rows_t.shape[0] // 2, weights_high.shape[2] // 2
    copies = []
    for h in range(2):
        left = rows_t[pl.ds(0, rows), :]
        value = dot(left, weights_high[h]) + dot(left, weights_low[h])
        staged[h, :, 0, :] = value[:, :columns]
        staged[h, :, 1, :] = -value[:, columns:]
        offset = lax.axis_index("core") * (block.shape[2] // 2) + h * columns
        copy = pltpu.make_async_copy(
            staged.at[h], block.at[:, :, pl.ds(pl.multiple_of(offset, columns), columns)], arrived.at[h]
        )
        copy.start()
        copies.append(copy)
    for copy in copies:
        copy.wait()


def keep_call(rows_t, weights_high, weights_low, width):
    rows, columns = rows_t.shape[0] // 2, weights_high.shape[2] // 2
    return pl.pallas_call(
        keep_kernel,
        out_shape=jax.ShapeDtypeStruct((rows, 2, width), jnp.float32),
        in_specs=[pl.BlockSpec(memory_space=pltpu.VMEM)] * 3,
        out_specs=pl.BlockSpec(memory_space=pltpu.HBM),
        scratch_shapes=[pltpu.VMEM((2, rows, 2, columns), jnp.float32), pltpu.SemaphoreType.DMA((2,))],
        compiler_params=pltpu.CompilerParams(vmem_limit_bytes=LIMIT),
        cost_estimate=pl.CostEstimate(flops=KEEP_COST, bytes_accessed=1024, transcendentals=0),
        name="keep",
    )(rows_t, weights_high, weights_low)


def place_kernel(_, *refs):
    sources, (block, staged, arrived) = refs[:-3], refs[-3:]
    columns = staged.shape[3]
    copies = []
    for number, source in enumerate(sources):
        staged[number, :, 0, :] = source[:, :columns]
        staged[number, :, 1, :] = source[:, columns:]
        offset = (1 - lax.axis_index("core")) * (block.shape[2] // 2) + number * columns
        copy = pltpu.make_async_copy(
            staged.at[number], block.at[:, :, pl.ds(pl.multiple_of(offset, columns), columns)], arrived.at[number]
        )
        copy.start()
        copies.append(copy)
    for copy in copies:
        copy.wait()


def place_call(block, got):
    rows, columns = got[0].shape
    return pl.pallas_call(
        place_kernel,
        out_shape=jax.ShapeDtypeStruct(block.shape, jnp.float32),
        in_specs=[pl.BlockSpec(memory_space=pltpu.HBM)] + [pl.BlockSpec(memory_space=pltpu.VMEM)] * len(got),
        out_specs=pl.BlockSpec(memory_space=pltpu.HBM),
        input_output_aliases={0: 0},
        scratch_shapes=[
            pltpu.VMEM((len(got), rows, 2, columns // 2), jnp.float32),
            pltpu.SemaphoreType.DMA((len(got),)),
        ],
        compiler_params=pltpu.CompilerParams(vmem_limit_bytes=LIMIT),
        name="place",
    )(block, *got)


def plain_gram(place, pieces, shots, rows):
    width = pieces[0].shape[1]
    even = jnp.concatenate(pieces, 0)
    turned = even.reshape(-1, 2, shots, width)
    odd = jnp.stack([-turned[:, 1], turned[:, 0]], 1).reshape(even.shape)
    blocks = []
    for number in range(2):
        blocks.append(lax.dynamic_slice_in_dim(even, place[number] * rows, rows, 1).T)
        blocks.append(-lax.dynamic_slice_in_dim(odd, place[number] * rows, rows, 1).T)
    return even, odd, 0.1 * jnp.sum(jnp.square(even.astype(jnp.float32))) / width, jnp.concatenate(blocks, 0)


def dot_tn(left, right):
    return lax.dot_general(left, right, (((0,), (0,)), ((), ())), preferred_element_type=jnp.float32)


def plain_apply(even, odd, parts):
    out = []
    for side in (even, odd):
        high, low = split(sum(dot_tn(side, part) for part in parts))
        out.append(dot(side, high) + dot(side, low))
    return out[0] + out[1]


def plain_solve(even, odd, damping, rows_t, pieces):
    start = jnp.concatenate(pieces, 0)
    wide = start.astype(jnp.float32)
    image = plain_apply(even, odd, (start,))
    norm_now = jnp.sum(wide * image, axis=0)
    alpha = norm_now / (jnp.sum(image * image, axis=0) + damping * norm_now)
    resid = (1.0 - alpha * damping) * wide - alpha * image
    resid_image = plain_apply(even, odd, split(resid))
    norm_next = jnp.sum(resid * resid_image, axis=0)
    ratio = norm_next / norm_now
    direc = resid + ratio * wide
    direc_image = resid_image + ratio * image
    curv = jnp.sum(direc_image * (direc_image + damping * direc), axis=0)
    weights_high, weights_low = split(alpha * wide + norm_next / curv * direc)
    block = (dot(rows_t, weights_high) + dot(rows_t, weights_low)).reshape(2, 2, -1, start.shape[1])
    return block[0], block[1]


def shards(up_traces, down_traces):
    local_shots, samples, width = up_traces.shape
    nfreq, chips = lax.axis_size("freq"), lax.axis_size("chip")
    core = lax.axis_index("core")
    half = width // 2
    rows = width // (2 * chips)
    size = 2 * local_shots * nfreq * 2 * chips
    matrix = jnp.asarray(spread_table(samples, nfreq, local_shots))

    down_spec = spectra(down_traces, matrix)
    up_spec = spectra(up_traces, after(matrix, down_spec))
    down = after(to_freq(down_spec, nfreq), up_spec)
    own = ring_gather(down, chips)

    up = to_freq(after(up_spec, down), nfreq)
    mine = lax.dynamic_slice_in_dim(up, core * half, half, 1)
    theirs = swap_core(lax.dynamic_slice_in_dim(up, (1 - core) * half, half, 1))
    up = jnp.concatenate([mine, theirs], 0)

    pieces = []
    for piece in own:
        pieces += [piece, swap_core(piece)]
    place = 2 * lax.axis_index("chip") + jnp.stack([core, 1 - core]).astype(jnp.int32)

    small = 2 * chips * 2 * local_shots * nfreq <= 1024 and rows == 128 and half == 2 * CHUNK and local_shots == 16
    if not small:
        operator = plain_gram(place, pieces, local_shots, rows)
        chunk = CHUNK if half % CHUNK == 0 else half
        kept, got = [], []
        for at in range(0, half, chunk):
            stay, send = plain_solve(*operator, ring_gather(up[:, at : at + chunk], chips))
            kept.append(stay)
            got.append(swap_core(send))
        kept, got = jnp.concatenate(kept, 2), jnp.concatenate(got, 2)
        first = core == 0
        block = jnp.concatenate([jnp.where(first, kept, got), jnp.where(first, got, kept)], 2)
        return jnp.transpose(block, (1, 0, 2))[None]

    operator = gram_call(place, pieces, local_shots, rows)
    gathered = ring_gather(up, chips, operator[2])
    early = stage_call(*operator[:2], gathered[:-1], local_shots)
    sent, *weights = solve_call(*operator, *early, gathered[-1], local_shots)
    got = swap_core(sent)
    return place_call(keep_call(operator[3], *weights, width), [got])[None]


def solution(mesh):
    nfreq, nshot = mesh.devices.shape
    fine = Mesh(mesh.devices.reshape(nfreq, nshot // 2, 2), ("freq", "chip", "core"))
    spec = P(("freq", "chip", "core"), None, None)
    out_specs = P("freq", ("chip", "core"), None, None)
    return jax.shard_map(shards, mesh=fine, in_specs=(spec, spec), out_specs=out_specs, check_vma=False)
```

```python
import functools
import math

import jax
import jax.numpy as jnp
import numpy as np
from jax import lax
from jax.experimental import pallas as pl
from jax.experimental.pallas import tpu as pltpu
from jax.sharding import Mesh, PartitionSpec as P

CHUNK = 256
LIMIT = 32 * 1024 * 1024
GRAM_COST = 4_000_000_000
SOLVE_COST = 1024
KEEP_COST = 1_000_000_000
STAGE_COST = 2_000_000_000


def make_table(samples, nfreq, first):
    times = np.arange(samples)
    phase = times[:, None] * (first + np.arange(nfreq))[None, :] % samples
    angle = np.float32(2.0 * math.pi) * phase.astype(np.float32) / np.float32(samples)
    return np.stack([np.cos(angle), -np.sin(angle)], -1).astype(jnp.bfloat16)


def spread_table(samples, nfreq, shots):
    table = make_table(samples, nfreq, samples // 16).astype(np.float32)
    whole = np.einsum("tfc,sz->fcszt", table, np.eye(shots, dtype=np.float32))
    return whole.reshape(nfreq * 2 * shots, shots * samples).astype(jnp.bfloat16)


def ring_order(chips):
    return [0, 1, 3, 2] if chips == 4 else list(range(chips))


def ring_gather(piece, chips, *before_last):
    order = ring_order(chips)
    pairs = [(order[i], order[(i + 1) % chips]) for i in range(chips)]
    if chips == 4:
        ahead = lax.ppermute(piece, "chip", pairs)
        back = lax.ppermute(piece, "chip", [(there, here) for here, there in pairs])
        return [piece, ahead, back, lax.ppermute(after(ahead, *before_last) if before_last else ahead, "chip", pairs)]
    pieces = [piece]
    for _ in range(1, chips):
        pieces.append(lax.ppermute(pieces[-1], "chip", pairs))
    return pieces


def after(array, *others):
    return lax.optimization_barrier((array, *others))[0]


def swap_core(array):
    return lax.ppermute(array, "core", [(0, 1), (1, 0)])


def split(array):
    high = lax.reduce_precision(array, 8, 7)
    return high.astype(jnp.bfloat16), (array - high).astype(jnp.bfloat16)


def dot(left, right):
    return jnp.dot(left, right, preferred_element_type=jnp.float32)


def dot_nt(left, right):
    return lax.dot_general(left, right, (((1,), (1,)), ((), ())), preferred_element_type=jnp.float32)


def spectra(traces, matrix):
    return dot(matrix, traces.reshape(-1, traces.shape[2])).astype(jnp.bfloat16)


def to_freq(spec, nfreq):
    parts = spec.reshape(nfreq, -1, spec.shape[1])
    me = lax.axis_index("freq")
    out = []
    for step in range(nfreq):
        there = me ^ step
        part = lax.dynamic_index_in_dim(parts, there, 0, keepdims=False)
        out.append(part if step == 0 else lax.ppermute(part, "freq", [(f, f ^ step) for f in range(nfreq)]))
    return jnp.concatenate(out, 0)


def gram_kernel(shots, place, *refs):
    pieces, (high, low, damping, rows_t), both = refs[:-5], refs[-5:-1], refs[-1]
    count, width = pieces[0].shape
    total = jnp.zeros((1, width), jnp.float32)
    for number, piece in enumerate(pieces):
        at = number // 2 * 2 * count + number % 2 * (count // 2)
        for part in range(0, count, 2 * shots):
            real, imag = piece[pl.ds(part, shots), :], piece[pl.ds(part + shots, shots), :]
            both[pl.ds(at, shots), pl.ds(0, width)] = real
            both[pl.ds(at, shots), pl.ds(width, width)] = -imag
            both[pl.ds(count + at, shots), pl.ds(0, width)] = imag
            both[pl.ds(count + at, shots), pl.ds(width, width)] = real
            real, imag = real.astype(jnp.float32), imag.astype(jnp.float32)
            total += jnp.sum(real * real + imag * imag, axis=0, keepdims=True)
            at += shots
    damping[...] = 0.1 * jnp.sum(total, axis=1, keepdims=True) / width
    left = jnp.concatenate([both[pl.ds(at, count), :] for at in range(0, both.shape[0], 2 * count)], 0)
    for at in range(0, left.shape[0], 256):
        gram = dot_nt(left[at : at + 256], both[...])
        rounded = gram.astype(jnp.bfloat16)
        high[pl.ds(at, 256), :] = rounded
        low[pl.ds(at, 256), :] = (gram - rounded.astype(jnp.float32)).astype(jnp.bfloat16)
    wide = rows_t.shape[0] // 2
    for number in range(2):
        start = pl.multiple_of(place[number] * wide, wide)
        rows_t[pl.ds(number * wide, wide), :] = both[:, pl.ds(start, wide)].T


def gram_call(place, pieces, shots, rows):
    count, width = pieces[0].shape
    size = count * len(pieces)
    block = jax.ShapeDtypeStruct((size // 2, size), jnp.bfloat16)
    return pl.pallas_call(
        functools.partial(gram_kernel, shots),
        out_shape=(
            block,
            block,
            jax.ShapeDtypeStruct((1, 1), jnp.float32),
            jax.ShapeDtypeStruct((2 * rows, size), jnp.bfloat16),
        ),
        in_specs=[pl.BlockSpec(memory_space=pltpu.SMEM)] + [pl.BlockSpec(memory_space=pltpu.VMEM)] * len(pieces),
        out_specs=(pl.BlockSpec(memory_space=pltpu.VMEM),) * 4,
        scratch_shapes=[pltpu.VMEM((size, 2 * width), jnp.bfloat16)],
        compiler_params=pltpu.CompilerParams(vmem_limit_bytes=LIMIT),
        cost_estimate=pl.CostEstimate(flops=GRAM_COST, bytes_accessed=1024, transcendentals=0),
        name="gram",
    )(place, *pieces)


def fill_turned(target, at, below, value):
    count, columns = value.shape[0], value.shape[1] // 2
    target[pl.ds(at, count), :] = value
    target[pl.ds(below, count), pl.ds(0, columns)] = value[:, columns:]
    target[pl.ds(below, count), pl.ds(columns, columns)] = -value[:, :columns]


def fill_piece(shots, source, first, target, number):
    count, columns = source.shape[0], target.shape[1] // 2
    at = number * count
    for part in range(0, count, 2 * shots):
        real, imag = (source[pl.ds(part + side, shots), pl.ds(first, columns)] for side in (0, shots))
        fill_turned(target, at, at + count // 2, jnp.concatenate([real, imag], 1))
        at += shots


def per_column(total):
    columns = total.shape[1] // 2
    total = total[:, :columns] + total[:, columns:]
    return jnp.concatenate([total, total], 1)


def two_parts(value):
    high = value.astype(jnp.bfloat16)
    return high, (value - high.astype(jnp.float32)).astype(jnp.bfloat16)


def taking_turns(*lists):
    for number in range(max(len(steps) for steps in lists)):
        for steps in lists:
            if number < len(steps):
                steps[number]()


class Half:
    def __init__(self, high, low, damping, early, earlier, late, image, step_high, step_low, step_image):
        self.high, self.low, self.damping = high, low, damping
        self.early, self.earlier, self.late, self.image = early, earlier, late, image
        self.step_high, self.step_low, self.step_image = step_high, step_low, step_image
        self.count, self.columns = late.shape[0] // 2, late.shape[1] // 2
        self.blocks = range(high.shape[0] // self.count)
        self.sums = [jnp.zeros((1, 2 * self.columns), jnp.float32) for _ in range(4)]

    def rows(self, block):
        return pl.ds(block * self.count, self.count)

    def add(self, which, value):
        self.sums[which] = self.sums[which] + jnp.sum(value, axis=0, keepdims=True)

    def begin(self, block):
        last = block == self.blocks[-1]
        ref, at = (self.late, 0) if last else (self.early, 2 * block * self.count)
        return ref[pl.ds(at, self.count), :].astype(jnp.float32)

    def store(self, block, value):
        at = 2 * block * self.count
        for target, part in zip((self.step_high, self.step_low), two_parts(value)):
            fill_turned(target, at, at + self.count, part)

    def apply_start(self):
        columns = pl.ds(self.early.shape[0], 2 * self.count)

        def step(block):
            rows = self.rows(block)
            value = self.earlier[rows, :] + (
                dot(self.high[rows, columns], self.late[...]) + dot(self.low[rows, columns], self.late[...])
            )
            self.image[rows, :] = value
            self.add(0, self.begin(block) * value)
            self.add(1, value * value)

        return [functools.partial(step, block) for block in self.blocks]

    def take_step(self):
        def scalars():
            self.norm_now, image_norm = per_column(self.sums[0]), per_column(self.sums[1])
            self.alpha = self.norm_now / (image_norm + self.damping * self.norm_now)
            self.keep = 1.0 - self.alpha * self.damping

        def step(block):
            resid = self.keep * self.begin(block) - self.alpha * self.image[self.rows(block), :]
            self.step_image[self.rows(block), :] = resid
            self.store(block, resid)

        return [scalars] + [functools.partial(step, block) for block in self.blocks]

    def apply_step(self):
        def step(block):
            rows = self.rows(block)
            value = dot(self.high[rows, :], self.step_high[...]) + (
                dot(self.low[rows, :], self.step_high[...]) + dot(self.high[rows, :], self.step_low[...])
            )
            self.add(2, self.step_image[rows, :] * value)
            self.step_image[rows, :] = value

        return [functools.partial(step, block) for block in self.blocks]

    def weigh(self):
        def scalars():
            self.norm_next = per_column(self.sums[2])
            self.ratio = self.norm_next / self.norm_now

        def curvature(block):
            rows = self.rows(block)
            image = self.image[rows, :]
            direc = (self.keep + self.ratio) * self.begin(block) - self.alpha * image
            value = self.step_image[rows, :] + self.ratio * image
            self.add(3, value * (value + self.damping * direc))

        def more_scalars():
            beta = self.norm_next / per_column(self.sums[3])
            self.from_start = self.alpha + beta * (self.keep + self.ratio)
            self.from_image = self.alpha * beta

        def step(block):
            self.store(block, self.from_start * self.begin(block) - self.from_image * self.image[self.rows(block), :])

        return (
            [scalars]
            + [functools.partial(curvature, block) for block in self.blocks]
            + [more_scalars]
            + [functools.partial(step, block) for block in self.blocks]
        )


def stage_kernel(shots, high, low, *refs):
    sources, (early, earlier) = refs[:-2], refs[-2:]
    columns, known = early.shape[2] // 2, pl.ds(0, early.shape[1])
    for h in range(2):
        for number, source in enumerate(sources):
            fill_piece(shots, source, h * columns, early.at[h], number)
    for h in range(2):
        for at in range(0, high.shape[0], 128):
            rows = pl.ds(at, 128)
            earlier[h, rows, :] = dot(high[rows, known], early[h]) + dot(low[rows, known], early[h])


def stage_call(high, low, pieces, shots):
    half = high.shape[0]
    rows, columns = pieces[0].shape
    return pl.pallas_call(
        functools.partial(stage_kernel, shots),
        out_shape=(
            jax.ShapeDtypeStruct((2, len(pieces) * rows, columns), jnp.bfloat16),
            jax.ShapeDtypeStruct((2, half, columns), jnp.float32),
        ),
        in_specs=[pl.BlockSpec(memory_space=pltpu.VMEM)] * (2 + len(pieces)),
        out_specs=(pl.BlockSpec(memory_space=pltpu.VMEM),) * 2,
        compiler_params=pltpu.CompilerParams(vmem_limit_bytes=LIMIT),
        cost_estimate=pl.CostEstimate(flops=STAGE_COST, bytes_accessed=1024, transcendentals=0),
        name="stage",
    )(high, low, *pieces)


def solve_kernel(
    shots, high, low, damping, rows_t, early, earlier, piece, sent, weights_high, weights_low, late, image, step_image
):
    columns = late.shape[2] // 2
    damp = damping[...]
    one, two = (
        Half(
            high, low, damp, *(ref.at[h] for ref in (early, earlier, late, image, weights_high, weights_low, step_image))
        )
        for h in range(2)
    )
    rows = rows_t.shape[0] // 2

    def project(h):
        def step():
            left = rows_t[pl.ds(rows, rows), :]
            value = dot(left, weights_high[h]) + dot(left, weights_low[h])
            sent[:, pl.ds(h * columns, columns)] = value[:, :columns].astype(sent.dtype)
            sent[:, pl.ds((2 + h) * columns, columns)] = (-value[:, columns:]).astype(sent.dtype)

        return [step]

    fill_piece(shots, piece, 0, late.at[0], 0)
    fill_piece(shots, piece, columns, late.at[1], 0)
    taking_turns(one.apply_start())
    taking_turns(two.apply_start(), one.take_step())
    taking_turns(one.apply_step(), two.take_step())
    taking_turns(two.apply_step(), one.weigh())
    taking_turns(project(0), two.weigh())
    taking_turns(project(1))


def solve_call(high, low, damping, rows_t, early, earlier, piece, shots):
    half, size = high.shape
    count, columns = piece.shape[0], piece.shape[1] // 2
    rows = rows_t.shape[0] // 2
    weights = jax.ShapeDtypeStruct((2, size, 2 * columns), jnp.bfloat16)
    return pl.pallas_call(
        functools.partial(solve_kernel, shots),
        out_shape=(jax.ShapeDtypeStruct((rows, 4 * columns), jnp.bfloat16), weights, weights),
        in_specs=[pl.BlockSpec(memory_space=pltpu.VMEM)] * 7,
        out_specs=(pl.BlockSpec(memory_space=pltpu.VMEM),) * 3,
        scratch_shapes=[
            pltpu.VMEM((2, count, 2 * columns), jnp.bfloat16),
            pltpu.VMEM((2, half, 2 * columns), jnp.float32),
            pltpu.VMEM((2, half, 2 * columns), jnp.float32),
        ],
        compiler_params=pltpu.CompilerParams(vmem_limit_bytes=LIMIT),
        cost_estimate=pl.CostEstimate(flops=SOLVE_COST, bytes_accessed=1024, transcendentals=0),
        name="solve",
    )(high, low, damping, rows_t, early, earlier, piece)


def keep_kernel(rows_t, weights_high, weights_low, block, staged, arrived):
    rows, columns = rows_t.shape[0] // 2, weights_high.shape[2] // 2
    copies = []
    for h in range(2):
        left = rows_t[pl.ds(0, rows), :]
        value = dot(left, weights_high[h]) + dot(left, weights_low[h])
        staged[h, :, 0, :] = value[:, :columns]
        staged[h, :, 1, :] = -value[:, columns:]
        offset = lax.axis_index("core") * (block.shape[2] // 2) + h * columns
        copy = pltpu.make_async_copy(
            staged.at[h], block.at[:, :, pl.ds(pl.multiple_of(offset, columns), columns)], arrived.at[h]
        )
        copy.start()
        copies.append(copy)
    for copy in copies:
        copy.wait()


def keep_call(rows_t, weights_high, weights_low, width):
    rows, columns = rows_t.shape[0] // 2, weights_high.shape[2] // 2
    return pl.pallas_call(
        keep_kernel,
        out_shape=jax.ShapeDtypeStruct((rows, 2, width), jnp.float32),
        in_specs=[pl.BlockSpec(memory_space=pltpu.VMEM)] * 3,
        out_specs=pl.BlockSpec(memory_space=pltpu.HBM),
        scratch_shapes=[pltpu.VMEM((2, rows, 2, columns), jnp.float32), pltpu.SemaphoreType.DMA((2,))],
        compiler_params=pltpu.CompilerParams(vmem_limit_bytes=LIMIT),
        cost_estimate=pl.CostEstimate(flops=KEEP_COST, bytes_accessed=1024, transcendentals=0),
        name="keep",
    )(rows_t, weights_high, weights_low)


def place_kernel(_, *refs):
    sources, (block, staged, arrived) = refs[:-3], refs[-3:]
    columns = staged.shape[3]
    copies = []
    for number, source in enumerate(sources):
        staged[number, :, 0, :] = source[:, :columns].astype(jnp.float32)
        staged[number, :, 1, :] = source[:, columns:].astype(jnp.float32)
        offset = (1 - lax.axis_index("core")) * (block.shape[2] // 2) + number * columns
        copy = pltpu.make_async_copy(
            staged.at[number], block.at[:, :, pl.ds(pl.multiple_of(offset, columns), columns)], arrived.at[number]
        )
        copy.start()
        copies.append(copy)
    for copy in copies:
        copy.wait()


def place_call(block, got):
    rows, columns = got[0].shape
    return pl.pallas_call(
        place_kernel,
        out_shape=jax.ShapeDtypeStruct(block.shape, jnp.float32),
        in_specs=[pl.BlockSpec(memory_space=pltpu.HBM)] + [pl.BlockSpec(memory_space=pltpu.VMEM)] * len(got),
        out_specs=pl.BlockSpec(memory_space=pltpu.HBM),
        input_output_aliases={0: 0},
        scratch_shapes=[
            pltpu.VMEM((len(got), rows, 2, columns // 2), jnp.float32),
            pltpu.SemaphoreType.DMA((len(got),)),
        ],
        compiler_params=pltpu.CompilerParams(vmem_limit_bytes=LIMIT),
        name="place",
    )(block, *got)


def plain_gram(place, pieces, shots, rows):
    width = pieces[0].shape[1]
    even = jnp.concatenate(pieces, 0)
    turned = even.reshape(-1, 2, shots, width)
    odd = jnp.stack([-turned[:, 1], turned[:, 0]], 1).reshape(even.shape)
    blocks = []
    for number in range(2):
        blocks.append(lax.dynamic_slice_in_dim(even, place[number] * rows, rows, 1).T)
        blocks.append(-lax.dynamic_slice_in_dim(odd, place[number] * rows, rows, 1).T)
    return even, odd, 0.1 * jnp.sum(jnp.square(even.astype(jnp.float32))) / width, jnp.concatenate(blocks, 0)


def dot_tn(left, right):
    return lax.dot_general(left, right, (((0,), (0,)), ((), ())), preferred_element_type=jnp.float32)


def plain_apply(even, odd, parts):
    out = []
    for side in (even, odd):
        high, low = split(sum(dot_tn(side, part) for part in parts))
        out.append(dot(side, high) + dot(side, low))
    return out[0] + out[1]


def plain_solve(even, odd, damping, rows_t, pieces):
    start = jnp.concatenate(pieces, 0)
    wide = start.astype(jnp.float32)
    image = plain_apply(even, odd, (start,))
    norm_now = jnp.sum(wide * image, axis=0)
    alpha = norm_now / (jnp.sum(image * image, axis=0) + damping * norm_now)
    resid = (1.0 - alpha * damping) * wide - alpha * image
    resid_image = plain_apply(even, odd, split(resid))
    norm_next = jnp.sum(resid * resid_image, axis=0)
    ratio = norm_next / norm_now
    direc = resid + ratio * wide
    direc_image = resid_image + ratio * image
    curv = jnp.sum(direc_image * (direc_image + damping * direc), axis=0)
    weights_high, weights_low = split(alpha * wide + norm_next / curv * direc)
    block = (dot(rows_t, weights_high) + dot(rows_t, weights_low)).reshape(2, 2, -1, start.shape[1])
    return block[0], block[1]


def shards(up_traces, down_traces):
    local_shots, samples, width = up_traces.shape
    nfreq, chips = lax.axis_size("freq"), lax.axis_size("chip")
    core = lax.axis_index("core")
    half = width // 2
    rows = width // (2 * chips)
    size = 2 * local_shots * nfreq * 2 * chips
    matrix = jnp.asarray(spread_table(samples, nfreq, local_shots))

    down_spec = spectra(down_traces, matrix)
    up_spec = spectra(up_traces, after(matrix, down_spec))
    down = after(to_freq(down_spec, nfreq), up_spec)
    own = ring_gather(down, chips)

    up = to_freq(after(up_spec, down), nfreq)
    mine = lax.dynamic_slice_in_dim(up, core * half, half, 1)
    theirs = swap_core(lax.dynamic_slice_in_dim(up, (1 - core) * half, half, 1))
    up = jnp.concatenate([mine, theirs], 0)

    pieces = []
    for piece in own:
        pieces += [piece, swap_core(piece)]
    place = 2 * lax.axis_index("chip") + jnp.stack([core, 1 - core]).astype(jnp.int32)

    small = 2 * chips * 2 * local_shots * nfreq <= 1024 and rows == 128 and half == 2 * CHUNK and local_shots == 16
    if not small:
        operator = plain_gram(place, pieces, local_shots, rows)
        chunk = CHUNK if half % CHUNK == 0 else half
        kept, got = [], []
        for at in range(0, half, chunk):
            stay, send = plain_solve(*operator, ring_gather(up[:, at : at + chunk], chips))
            kept.append(stay)
            got.append(swap_core(send))
        kept, got = jnp.concatenate(kept, 2), jnp.concatenate(got, 2)
        first = core == 0
        block = jnp.concatenate([jnp.where(first, kept, got), jnp.where(first, got, kept)], 2)
        return jnp.transpose(block, (1, 0, 2))[None]

    operator = gram_call(place, pieces, local_shots, rows)
    gathered = ring_gather(up, chips)
    early = stage_call(*operator[:2], gathered[:-1], local_shots)
    sent, *weights = solve_call(*operator, *early, gathered[-1], local_shots)
    got = swap_core(sent)
    return place_call(keep_call(operator[3], *weights, width), [got])[None]


def solution(mesh):
    nfreq, nshot = mesh.devices.shape
    fine = Mesh(mesh.devices.reshape(nfreq, nshot // 2, 2), ("freq", "chip", "core"))
    spec = P(("freq", "chip", "core"), None, None)
    out_specs = P("freq", ("chip", "core"), None, None)
    return jax.shard_map(shards, mesh=fine, in_specs=(spec, spec), out_specs=out_specs, check_vma=False)
```

```python
import functools
import math

import jax
import jax.numpy as jnp
import numpy as np
from jax import lax
from jax.experimental import pallas as pl
from jax.experimental.pallas import tpu as pltpu
from jax.sharding import Mesh, PartitionSpec as P

CHUNK = 256
LIMIT = 32 * 1024 * 1024
GRAM_COST = 4_000_000_000
SOLVE_COST = 1024
KEEP_COST = 1_000_000_000
STAGE_COST = 20_000_000_000


def make_table(samples, nfreq, first):
    times = np.arange(samples)
    phase = times[:, None] * (first + np.arange(nfreq))[None, :] % samples
    angle = np.float32(2.0 * math.pi) * phase.astype(np.float32) / np.float32(samples)
    return np.stack([np.cos(angle), -np.sin(angle)], -1).astype(jnp.bfloat16)


def spread_table(samples, nfreq, shots):
    table = make_table(samples, nfreq, samples // 16).astype(np.float32)
    whole = np.einsum("tfc,sz->fcszt", table, np.eye(shots, dtype=np.float32))
    return whole.reshape(nfreq * 2 * shots, shots * samples).astype(jnp.bfloat16)


def ring_order(chips):
    return [0, 1, 3, 2] if chips == 4 else list(range(chips))


def ring_gather(piece, chips, *before_last):
    order = ring_order(chips)
    pairs = [(order[i], order[(i + 1) % chips]) for i in range(chips)]
    if chips == 4:
        ahead = lax.ppermute(piece, "chip", pairs)
        back = lax.ppermute(piece, "chip", [(there, here) for here, there in pairs])
        return [piece, ahead, back, lax.ppermute(after(ahead, *before_last) if before_last else ahead, "chip", pairs)]
    pieces = [piece]
    for _ in range(1, chips):
        pieces.append(lax.ppermute(pieces[-1], "chip", pairs))
    return pieces


def after(array, *others):
    return lax.optimization_barrier((array, *others))[0]


def swap_core(array):
    return lax.ppermute(array, "core", [(0, 1), (1, 0)])


def split(array):
    high = lax.reduce_precision(array, 8, 7)
    return high.astype(jnp.bfloat16), (array - high).astype(jnp.bfloat16)


def dot(left, right):
    return jnp.dot(left, right, preferred_element_type=jnp.float32)


def dot_nt(left, right):
    return lax.dot_general(left, right, (((1,), (1,)), ((), ())), preferred_element_type=jnp.float32)


def spectra(traces, matrix):
    return dot(matrix, traces.reshape(-1, traces.shape[2])).astype(jnp.bfloat16)


def to_freq(spec, nfreq):
    parts = spec.reshape(nfreq, -1, spec.shape[1])
    me = lax.axis_index("freq")
    out = []
    for step in range(nfreq):
        there = me ^ step
        part = lax.dynamic_index_in_dim(parts, there, 0, keepdims=False)
        out.append(part if step == 0 else lax.ppermute(part, "freq", [(f, f ^ step) for f in range(nfreq)]))
    return jnp.concatenate(out, 0)


def gram_kernel(shots, place, *refs):
    pieces, (high, low, damping, rows_t), both = refs[:-5], refs[-5:-1], refs[-1]
    count, width = pieces[0].shape
    total = jnp.zeros((1, width), jnp.float32)
    for number, piece in enumerate(pieces):
        at = number // 2 * 2 * count + number % 2 * (count // 2)
        for part in range(0, count, 2 * shots):
            real, imag = piece[pl.ds(part, shots), :], piece[pl.ds(part + shots, shots), :]
            both[pl.ds(at, shots), pl.ds(0, width)] = real
            both[pl.ds(at, shots), pl.ds(width, width)] = -imag
            both[pl.ds(count + at, shots), pl.ds(0, width)] = imag
            both[pl.ds(count + at, shots), pl.ds(width, width)] = real
            real, imag = real.astype(jnp.float32), imag.astype(jnp.float32)
            total += jnp.sum(real * real + imag * imag, axis=0, keepdims=True)
            at += shots
    damping[...] = 0.1 * jnp.sum(total, axis=1, keepdims=True) / width
    left = jnp.concatenate([both[pl.ds(at, count), :] for at in range(0, both.shape[0], 2 * count)], 0)
    for at in range(0, left.shape[0], 256):
        gram = dot_nt(left[at : at + 256], both[...])
        rounded = gram.astype(jnp.bfloat16)
        high[pl.ds(at, 256), :] = rounded
        low[pl.ds(at, 256), :] = (gram - rounded.astype(jnp.float32)).astype(jnp.bfloat16)
    wide = rows_t.shape[0] // 2
    for number in range(2):
        start = pl.multiple_of(place[number] * wide, wide)
        rows_t[pl.ds(number * wide, wide), :] = both[:, pl.ds(start, wide)].T


def gram_call(place, pieces, shots, rows):
    count, width = pieces[0].shape
    size = count * len(pieces)
    block = jax.ShapeDtypeStruct((size // 2, size), jnp.bfloat16)
    return pl.pallas_call(
        functools.partial(gram_kernel, shots),
        out_shape=(
            block,
            block,
            jax.ShapeDtypeStruct((1, 1), jnp.float32),
            jax.ShapeDtypeStruct((2 * rows, size), jnp.bfloat16),
        ),
        in_specs=[pl.BlockSpec(memory_space=pltpu.SMEM)] + [pl.BlockSpec(memory_space=pltpu.VMEM)] * len(pieces),
        out_specs=(pl.BlockSpec(memory_space=pltpu.VMEM),) * 4,
        scratch_shapes=[pltpu.VMEM((size, 2 * width), jnp.bfloat16)],
        compiler_params=pltpu.CompilerParams(vmem_limit_bytes=LIMIT),
        cost_estimate=pl.CostEstimate(flops=GRAM_COST, bytes_accessed=1024, transcendentals=0),
        name="gram",
    )(place, *pieces)


def fill_turned(target, at, below, value):
    count, columns = value.shape[0], value.shape[1] // 2
    target[pl.ds(at, count), :] = value
    target[pl.ds(below, count), pl.ds(0, columns)] = value[:, columns:]
    target[pl.ds(below, count), pl.ds(columns, columns)] = -value[:, :columns]


def fill_piece(shots, source, first, target, number):
    count, columns = source.shape[0], target.shape[1] // 2
    at = number * count
    for part in range(0, count, 2 * shots):
        real, imag = (source[pl.ds(part + side, shots), pl.ds(first, columns)] for side in (0, shots))
        fill_turned(target, at, at + count // 2, jnp.concatenate([real, imag], 1))
        at += shots


def per_column(total):
    columns = total.shape[1] // 2
    total = total[:, :columns] + total[:, columns:]
    return jnp.concatenate([total, total], 1)


def two_parts(value):
    high = value.astype(jnp.bfloat16)
    return high, (value - high.astype(jnp.float32)).astype(jnp.bfloat16)


def taking_turns(*lists):
    for number in range(max(len(steps) for steps in lists)):
        for steps in lists:
            if number < len(steps):
                steps[number]()


class Half:
    def __init__(self, high, low, damping, early, earlier, late, image, step_high, step_low, step_image):
        self.high, self.low, self.damping = high, low, damping
        self.early, self.earlier, self.late, self.image = early, earlier, late, image
        self.step_high, self.step_low, self.step_image = step_high, step_low, step_image
        self.count, self.columns = late.shape[0] // 2, late.shape[1] // 2
        self.blocks = range(high.shape[0] // self.count)
        self.sums = [jnp.zeros((1, 2 * self.columns), jnp.float32) for _ in range(4)]

    def rows(self, block):
        return pl.ds(block * self.count, self.count)

    def add(self, which, value):
        self.sums[which] = self.sums[which] + jnp.sum(value, axis=0, keepdims=True)

    def begin(self, block):
        last = block == self.blocks[-1]
        ref, at = (self.late, 0) if last else (self.early, 2 * block * self.count)
        return ref[pl.ds(at, self.count), :].astype(jnp.float32)

    def store(self, block, value):
        at = 2 * block * self.count
        for target, part in zip((self.step_high, self.step_low), two_parts(value)):
            fill_turned(target, at, at + self.count, part)

    def apply_start(self):
        columns = pl.ds(self.early.shape[0], 2 * self.count)

        def step(block):
            rows = self.rows(block)
            value = self.earlier[rows, :] + (
                dot(self.high[rows, columns], self.late[...]) + dot(self.low[rows, columns], self.late[...])
            )
            self.image[rows, :] = value
            self.add(0, self.begin(block) * value)
            self.add(1, value * value)

        return [functools.partial(step, block) for block in self.blocks]

    def take_step(self):
        def scalars():
            self.norm_now, image_norm = per_column(self.sums[0]), per_column(self.sums[1])
            self.alpha = self.norm_now / (image_norm + self.damping * self.norm_now)
            self.keep = 1.0 - self.alpha * self.damping

        def step(block):
            resid = self.keep * self.begin(block) - self.alpha * self.image[self.rows(block), :]
            self.step_image[self.rows(block), :] = resid
            self.store(block, resid)

        return [scalars] + [functools.partial(step, block) for block in self.blocks]

    def apply_step(self):
        def step(block):
            rows = self.rows(block)
            value = dot(self.high[rows, :], self.step_high[...]) + (
                dot(self.low[rows, :], self.step_high[...]) + dot(self.high[rows, :], self.step_low[...])
            )
            self.add(2, self.step_image[rows, :] * value)
            self.step_image[rows, :] = value

        return [functools.partial(step, block) for block in self.blocks]

    def weigh(self):
        def scalars():
            self.norm_next = per_column(self.sums[2])
            self.ratio = self.norm_next / self.norm_now

        def curvature(block):
            rows = self.rows(block)
            image = self.image[rows, :]
            direc = (self.keep + self.ratio) * self.begin(block) - self.alpha * image
            value = self.step_image[rows, :] + self.ratio * image
            self.add(3, value * (value + self.damping * direc))

        def more_scalars():
            beta = self.norm_next / per_column(self.sums[3])
            self.from_start = self.alpha + beta * (self.keep + self.ratio)
            self.from_image = self.alpha * beta

        def step(block):
            self.store(block, self.from_start * self.begin(block) - self.from_image * self.image[self.rows(block), :])

        return (
            [scalars]
            + [functools.partial(curvature, block) for block in self.blocks]
            + [more_scalars]
            + [functools.partial(step, block) for block in self.blocks]
        )


def stage_kernel(shots, high, low, *refs):
    sources, (early, earlier) = refs[:-2], refs[-2:]
    columns, known = early.shape[2] // 2, pl.ds(0, early.shape[1])
    for h in range(2):
        for number, source in enumerate(sources):
            fill_piece(shots, source, h * columns, early.at[h], number)
    for h in range(2):
        for at in range(0, high.shape[0], 128):
            rows = pl.ds(at, 128)
            earlier[h, rows, :] = dot(high[rows, known], early[h]) + dot(low[rows, known], early[h])


def stage_call(high, low, pieces, shots):
    half = high.shape[0]
    rows, columns = pieces[0].shape
    return pl.pallas_call(
        functools.partial(stage_kernel, shots),
        out_shape=(
            jax.ShapeDtypeStruct((2, len(pieces) * rows, columns), jnp.bfloat16),
            jax.ShapeDtypeStruct((2, half, columns), jnp.float32),
        ),
        in_specs=[pl.BlockSpec(memory_space=pltpu.VMEM)] * (2 + len(pieces)),
        out_specs=(pl.BlockSpec(memory_space=pltpu.VMEM),) * 2,
        compiler_params=pltpu.CompilerParams(vmem_limit_bytes=LIMIT),
        cost_estimate=pl.CostEstimate(flops=STAGE_COST, bytes_accessed=1024, transcendentals=0),
        name="stage",
    )(high, low, *pieces)


def solve_kernel(
    shots, high, low, damping, rows_t, early, earlier, piece, sent, weights_high, weights_low, late, image, step_image
):
    columns = late.shape[2] // 2
    damp = damping[...]
    one, two = (
        Half(
            high, low, damp, *(ref.at[h] for ref in (early, earlier, late, image, weights_high, weights_low, step_image))
        )
        for h in range(2)
    )
    rows = rows_t.shape[0] // 2

    def project(h):
        def step():
            left = rows_t[pl.ds(rows, rows), :]
            value = dot(left, weights_high[h]) + dot(left, weights_low[h])
            sent[:, pl.ds(h * columns, columns)] = value[:, :columns].astype(sent.dtype)
            sent[:, pl.ds((2 + h) * columns, columns)] = (-value[:, columns:]).astype(sent.dtype)

        return [step]

    fill_piece(shots, piece, 0, late.at[0], 0)
    fill_piece(shots, piece, columns, late.at[1], 0)
    taking_turns(one.apply_start())
    taking_turns(two.apply_start(), one.take_step())
    taking_turns(one.apply_step(), two.take_step())
    taking_turns(two.apply_step(), one.weigh())
    taking_turns(project(0), two.weigh())
    taking_turns(project(1))


def solve_call(high, low, damping, rows_t, early, earlier, piece, shots):
    half, size = high.shape
    count, columns = piece.shape[0], piece.shape[1] // 2
    rows = rows_t.shape[0] // 2
    weights = jax.ShapeDtypeStruct((2, size, 2 * columns), jnp.bfloat16)
    return pl.pallas_call(
        functools.partial(solve_kernel, shots),
        out_shape=(jax.ShapeDtypeStruct((rows, 4 * columns), jnp.bfloat16), weights, weights),
        in_specs=[pl.BlockSpec(memory_space=pltpu.VMEM)] * 7,
        out_specs=(pl.BlockSpec(memory_space=pltpu.VMEM),) * 3,
        scratch_shapes=[
            pltpu.VMEM((2, count, 2 * columns), jnp.bfloat16),
            pltpu.VMEM((2, half, 2 * columns), jnp.float32),
            pltpu.VMEM((2, half, 2 * columns), jnp.float32),
        ],
        compiler_params=pltpu.CompilerParams(vmem_limit_bytes=LIMIT),
        cost_estimate=pl.CostEstimate(flops=SOLVE_COST, bytes_accessed=1024, transcendentals=0),
        name="solve",
    )(high, low, damping, rows_t, early, earlier, piece)


def keep_kernel(rows_t, weights_high, weights_low, block, staged, arrived):
    rows, columns = rows_t.shape[0] // 2, weights_high.shape[2] // 2
    copies = []
    for h in range(2):
        left = rows_t[pl.ds(0, rows), :]
        value = dot(left, weights_high[h]) + dot(left, weights_low[h])
        staged[h, :, 0, :] = value[:, :columns]
        staged[h, :, 1, :] = -value[:, columns:]
        offset = lax.axis_index("core") * (block.shape[2] // 2) + h * columns
        copy = pltpu.make_async_copy(
            staged.at[h], block.at[:, :, pl.ds(pl.multiple_of(offset, columns), columns)], arrived.at[h]
        )
        copy.start()
        copies.append(copy)
    for copy in copies:
        copy.wait()


def keep_call(rows_t, weights_high, weights_low, width):
    rows, columns = rows_t.shape[0] // 2, weights_high.shape[2] // 2
    return pl.pallas_call(
        keep_kernel,
        out_shape=jax.ShapeDtypeStruct((rows, 2, width), jnp.float32),
        in_specs=[pl.BlockSpec(memory_space=pltpu.VMEM)] * 3,
        out_specs=pl.BlockSpec(memory_space=pltpu.HBM),
        scratch_shapes=[pltpu.VMEM((2, rows, 2, columns), jnp.float32), pltpu.SemaphoreType.DMA((2,))],
        compiler_params=pltpu.CompilerParams(vmem_limit_bytes=LIMIT),
        cost_estimate=pl.CostEstimate(flops=KEEP_COST, bytes_accessed=1024, transcendentals=0),
        name="keep",
    )(rows_t, weights_high, weights_low)


def place_kernel(_, *refs):
    sources, (block, staged, arrived) = refs[:-3], refs[-3:]
    columns = staged.shape[3]
    copies = []
    for number, source in enumerate(sources):
        staged[number, :, 0, :] = source[:, :columns].astype(jnp.float32)
        staged[number, :, 1, :] = source[:, columns:].astype(jnp.float32)
        offset = (1 - lax.axis_index("core")) * (block.shape[2] // 2) + number * columns
        copy = pltpu.make_async_copy(
            staged.at[number], block.at[:, :, pl.ds(pl.multiple_of(offset, columns), columns)], arrived.at[number]
        )
        copy.start()
        copies.append(copy)
    for copy in copies:
        copy.wait()


def place_call(block, got):
    rows, columns = got[0].shape
    return pl.pallas_call(
        place_kernel,
        out_shape=jax.ShapeDtypeStruct(block.shape, jnp.float32),
        in_specs=[pl.BlockSpec(memory_space=pltpu.HBM)] + [pl.BlockSpec(memory_space=pltpu.VMEM)] * len(got),
        out_specs=pl.BlockSpec(memory_space=pltpu.HBM),
        input_output_aliases={0: 0},
        scratch_shapes=[
            pltpu.VMEM((len(got), rows, 2, columns // 2), jnp.float32),
            pltpu.SemaphoreType.DMA((len(got),)),
        ],
        compiler_params=pltpu.CompilerParams(vmem_limit_bytes=LIMIT),
        name="place",
    )(block, *got)


def plain_gram(place, pieces, shots, rows):
    width = pieces[0].shape[1]
    even = jnp.concatenate(pieces, 0)
    turned = even.reshape(-1, 2, shots, width)
    odd = jnp.stack([-turned[:, 1], turned[:, 0]], 1).reshape(even.shape)
    blocks = []
    for number in range(2):
        blocks.append(lax.dynamic_slice_in_dim(even, place[number] * rows, rows, 1).T)
        blocks.append(-lax.dynamic_slice_in_dim(odd, place[number] * rows, rows, 1).T)
    return even, odd, 0.1 * jnp.sum(jnp.square(even.astype(jnp.float32))) / width, jnp.concatenate(blocks, 0)


def dot_tn(left, right):
    return lax.dot_general(left, right, (((0,), (0,)), ((), ())), preferred_element_type=jnp.float32)


def plain_apply(even, odd, parts):
    out = []
    for side in (even, odd):
        high, low = split(sum(dot_tn(side, part) for part in parts))
        out.append(dot(side, high) + dot(side, low))
    return out[0] + out[1]


def plain_solve(even, odd, damping, rows_t, pieces):
    start = jnp.concatenate(pieces, 0)
    wide = start.astype(jnp.float32)
    image = plain_apply(even, odd, (start,))
    norm_now = jnp.sum(wide * image, axis=0)
    alpha = norm_now / (jnp.sum(image * image, axis=0) + damping * norm_now)
    resid = (1.0 - alpha * damping) * wide - alpha * image
    resid_image = plain_apply(even, odd, split(resid))
    norm_next = jnp.sum(resid * resid_image, axis=0)
    ratio = norm_next / norm_now
    direc = resid + ratio * wide
    direc_image = resid_image + ratio * image
    curv = jnp.sum(direc_image * (direc_image + damping * direc), axis=0)
    weights_high, weights_low = split(alpha * wide + norm_next / curv * direc)
    block = (dot(rows_t, weights_high) + dot(rows_t, weights_low)).reshape(2, 2, -1, start.shape[1])
    return block[0], block[1]


def shards(up_traces, down_traces):
    local_shots, samples, width = up_traces.shape
    nfreq, chips = lax.axis_size("freq"), lax.axis_size("chip")
    core = lax.axis_index("core")
    half = width // 2
    rows = width // (2 * chips)
    size = 2 * local_shots * nfreq * 2 * chips
    matrix = jnp.asarray(spread_table(samples, nfreq, local_shots))

    down_spec = spectra(down_traces, matrix)
    up_spec = spectra(up_traces, after(matrix, down_spec))
    down = after(to_freq(down_spec, nfreq), up_spec)
    own = ring_gather(down, chips)

    up = to_freq(after(up_spec, down), nfreq)
    mine = lax.dynamic_slice_in_dim(up, core * half, half, 1)
    theirs = swap_core(lax.dynamic_slice_in_dim(up, (1 - core) * half, half, 1))
    up = jnp.concatenate([mine, theirs], 0)

    pieces = []
    for piece in own:
        pieces += [piece, swap_core(piece)]
    place = 2 * lax.axis_index("chip") + jnp.stack([core, 1 - core]).astype(jnp.int32)

    small = 2 * chips * 2 * local_shots * nfreq <= 1024 and rows == 128 and half == 2 * CHUNK and local_shots == 16
    if not small:
        operator = plain_gram(place, pieces, local_shots, rows)
        chunk = CHUNK if half % CHUNK == 0 else half
        kept, got = [], []
        for at in range(0, half, chunk):
            stay, send = plain_solve(*operator, ring_gather(up[:, at : at + chunk], chips))
            kept.append(stay)
            got.append(swap_core(send))
        kept, got = jnp.concatenate(kept, 2), jnp.concatenate(got, 2)
        first = core == 0
        block = jnp.concatenate([jnp.where(first, kept, got), jnp.where(first, got, kept)], 2)
        return jnp.transpose(block, (1, 0, 2))[None]

    operator = gram_call(place, pieces, local_shots, rows)
    gathered = ring_gather(up, chips)
    early = stage_call(*operator[:2], gathered[:-1], local_shots)
    sent, *weights = solve_call(*operator, *early, gathered[-1], local_shots)
    got = swap_core(sent)
    return place_call(keep_call(operator[3], *weights, width), [got])[None]


def solution(mesh):
    nfreq, nshot = mesh.devices.shape
    fine = Mesh(mesh.devices.reshape(nfreq, nshot // 2, 2), ("freq", "chip", "core"))
    spec = P(("freq", "chip", "core"), None, None)
    out_specs = P("freq", ("chip", "core"), None, None)
    return jax.shard_map(shards, mesh=fine, in_specs=(spec, spec), out_specs=out_specs, check_vma=False)
```
